128 devices in a mesh: wide: 16 (over z_lo, y, core), narrow: 8 (over z_hi, x).
Axes of the slice: x: 4, y: 4, z: 4 (z_hi: 2, z_lo: 2; z = z_hi * 2 + z_lo), core: 2. Of those that a mesh axis runs over, the one named last changes fastest.
Arguments:
- trajectory: bfloat16 [5, 72, 512, 2048], P(None, None, 'narrow', 'wide'), may hold values from -6 to 6
- innovation: float32 [5, 72, 128, 512], P(None, None, 'narrow', 'wide'), may hold values from -6 to 6
- background: float32 [5, 72, 128, 512], P(None, None, 'narrow', 'wide'), may hold values from -6 to 6
- obs_weight: float32 [72, 128, 512], P(None, 'narrow', 'wide'), may hold values from 0.3 to 3
Outputs:
- analysis: bfloat16 [5, 72, 512, 2048], P(None, None, 'narrow', 'wide')
The draws below stay inside these ranges and needn't reach their ends.
All inputs are finite; a program needn't handle non-finite values.
Results may differ from the reference program's by a relative error of at most 0.001.
Values sent between devices are 32-bit elements; how exact they have to be, the bound alone decides.
No kernel may reach another device: no remote copies, remote signals or barrier semaphores. Data moves between devices by JAX's collectives and lax.ppermute only.
A program may use at most 128 MiB of HBM per device.

```python
import math
import jax
import jax.numpy as jnp
from jax import lax

FIELDS = 5
LEVELS = 72
COARSEN = 4
STEPS = 2
ITERS = 1
NLAT = 512
NLON = 2048
NLAT_C = 128
NLON_C = 512


def levels(stream_key, dims, pieces, least, largest):
    factor_of = 1.0
    for axis_at, blocks in pieces:
        draws = jax.random.uniform(jax.random.fold_in(jax.random.fold_in(stream_key, 6), axis_at), (blocks,), jnp.float32, least / len(pieces), largest / len(pieces))
        factor_of = factor_of * jnp.repeat(jnp.exp(draws), dims[axis_at] // blocks).reshape((-1,) + (1,) * (len(dims) - 1 - axis_at))
    return factor_of


def normal_values(rng, extent, deviation, most, split=(), kind=jnp.bfloat16):
    level = levels(rng, extent, split, -0.22, 0.18) if split else 1.0
    drawn = jax.random.normal(rng, extent, jnp.float32) * deviation * level
    return jnp.minimum(jnp.maximum(drawn, -most), most).astype(kind)


def setup_inputs(seed: int = 0) -> dict:
    arg_keys = jax.random.split(jax.random.key(seed), 5)
    return {
        "trajectory": normal_values(arg_keys[0], (FIELDS, LEVELS, NLAT, NLON), 1.0, 6.0, ((2, 8), (3, 16))),
        "innovation": normal_values(arg_keys[1], (FIELDS, LEVELS, NLAT_C, NLON_C), 1.0, 6.0, ((2, 8), (3, 16)), jnp.float32),
        "background": normal_values(arg_keys[2], (FIELDS, LEVELS, NLAT_C, NLON_C), 0.7, 6.0, ((2, 8), (3, 16)), jnp.float32),
        "obs_weight": jnp.clip(jnp.exp(math.log(3.0) - 2.3025851 * jax.random.uniform(arg_keys[3], (LEVELS, NLAT_C, NLON_C), jnp.float32) ** levels(arg_keys[3], (LEVELS, NLAT_C, NLON_C), ((1, 8), (2, 16)), -0.2, 0.2)), 0.3, 3.0),
    }


diffusion = 0.2
advection_scale = 0.3
descent_step = 1.0


def filter_rows(row_index, total_rows, cycle_size):
    wavenumber = jnp.arange(cycle_size, dtype=jnp.int32)
    folded = jnp.minimum(wavenumber, cycle_size - wavenumber).astype(jnp.float32)
    latitude = jnp.pi * ((row_index.astype(jnp.float32) + 0.5) / total_rows - 0.5)
    cutoff = 0.5 * cycle_size * jnp.cos(latitude)
    scaled_wave = folded[None, :] / cutoff[:, None]
    response = 1.0 / (1.0 + scaled_wave ** 4)
    phase_index = (wavenumber[:, None] * wavenumber[None, :]) % cycle_size
    angles = (2.0 * jnp.pi / cycle_size) * phase_index.astype(jnp.float32)
    basis = jnp.concatenate([jnp.cos(angles), jnp.sin(angles)], axis=0)
    doubled = jnp.concatenate([response, response], axis=1)
    weighted = doubled[:, :, None] * basis[None]
    return jnp.einsum("rka,kb->rab", weighted, basis, precision=lax.Precision.HIGHEST) / cycle_size


def tangent_step(model_state, extend_rows, drift_coef, kernel):
    padded = extend_rows(model_state)
    north_row = padded[:, :, :-2]
    south_row = padded[:, :, 2:]
    east_cell = jnp.roll(model_state, -1, axis=3)
    west_cell = jnp.roll(model_state, 1, axis=3)
    updated = model_state + diffusion * (north_row + south_row + east_cell + west_cell - 4.0 * model_state) + drift_coef * (east_cell - west_cell)
    return jnp.einsum("flrb,rbc->flrc", updated, kernel, precision=lax.Precision.HIGHEST)


def adjoint_step(costate, extend_rows, drift_coef, kernel):
    filtered = jnp.einsum("flrb,rbc->flrc", costate, kernel, precision=lax.Precision.HIGHEST)
    padded = extend_rows(filtered)
    north_row = padded[:, :, :-2]
    south_row = padded[:, :, 2:]
    east_cell = jnp.roll(filtered, -1, axis=3)
    west_cell = jnp.roll(filtered, 1, axis=3)
    carried = drift_coef * filtered
    return filtered + diffusion * (north_row + south_row + east_cell + west_cell - 4.0 * filtered) + jnp.roll(carried, 1, axis=3) - jnp.roll(carried, -1, axis=3)


def pad_rows(model_state):
    return jnp.pad(model_state, ((0, 0), (0, 0), (1, 1), (0, 0)))


def reference(trajectory, innovation, background, obs_weight):
    coarse_rows = NLAT_C
    cycle_size = NLON_C
    zonal_wind = trajectory[0].astype(jnp.float32).reshape(LEVELS, coarse_rows, COARSEN, cycle_size, COARSEN)
    zonal_wind = jnp.mean(zonal_wind, axis=(2, 4))
    drift_coef = (advection_scale * jnp.tanh(zonal_wind))[None]
    kernel = filter_rows(jnp.arange(coarse_rows, dtype=jnp.int32), coarse_rows, cycle_size)
    increment = background
    for outer_turn in range(ITERS):
        model_state = increment
        for step_index in range(STEPS):
            model_state = tangent_step(model_state, pad_rows, drift_coef, kernel)
        costate = obs_weight[None] * (model_state - innovation)
        for step_index in range(STEPS):
            costate = adjoint_step(costate, pad_rows, drift_coef, kernel)
        increment = increment - descent_step * (increment - background + costate)

    def finish(field_pair):
        layer_field, coarse_part = field_pair
        fine_part = jnp.repeat(jnp.repeat(coarse_part, COARSEN, axis=2), COARSEN, axis=1)
        return (layer_field.astype(jnp.float32) + fine_part).astype(jnp.bfloat16)

    return lax.map(finish, (trajectory, increment))
```

```python
import jax
import jax.numpy as jnp
import ml_dtypes
import numpy as np
from jax import lax
from jax.experimental import pallas as pl
from jax.experimental.pallas import tpu as pltpu
from jax.sharding import PartitionSpec as P

FIELDS = 5
LEVELS = 72
COARSEN = 4
ROWS = 16
COLS = 32
CYCLE = 512
HALF = 256
TOTAL_ROWS = 128
SHARE = 5
GROUP = 32
PLANES = FIELDS * SHARE
WIDE = 16
HALO = 4
BAND = ROWS + 2 * HALO

diffusion = 0.2
advection_scale = 0.3
MIB = 2**20


def harmonics():
    column = np.arange(HALF)

    def wave(function, wavenumbers):
        angle = 2 * np.pi * ((column[:, None] * wavenumbers[None, :]) % CYCLE) / CYCLE
        scale = np.where((wavenumbers == 0) | (wavenumbers == HALF), 1.0, 2.0)
        return function(angle) * np.sqrt(scale / CYCLE)

    even_cos, even_sin = np.arange(0, HALF + 1, 2), np.arange(2, HALF, 2)
    odd = np.arange(1, HALF, 2)
    even = np.concatenate([wave(np.cos, even_cos), wave(np.sin, even_sin)], axis=1)
    odds = np.concatenate([wave(np.cos, odd), wave(np.sin, odd)], axis=1)
    order = np.concatenate([even_cos, even_sin, odd, odd])
    return even, odds, order


def stacked(matrix):
    high = matrix.astype(ml_dtypes.bfloat16)
    low = (matrix - high.astype(np.float64)).astype(ml_dtypes.bfloat16)
    return np.concatenate([high, high, low], axis=0)


EVEN, ODD, WAVES = harmonics()
BASIS = np.stack([stacked(EVEN), stacked(ODD), stacked(EVEN.T), stacked(ODD.T)])


def pooling():
    fine = np.arange(4 * COLS)
    matrix = np.zeros((4, 4 * COLS, 4 * COLS), np.float32)
    for part in range(4):
        matrix[part, fine, part * COLS + fine // 4] = 1.0 / 16
    return matrix.reshape(4 * 4 * COLS, 4 * COLS)


def spreading():
    fine = np.arange(4 * COLS)
    matrix = np.zeros((4 * COLS, 4, 4 * COLS), np.float32)
    for part in range(4):
        matrix[part * COLS + fine // 4, part, fine] = 1.0
    matrix = matrix.reshape(4 * COLS, 16 * COLS)
    return np.concatenate([matrix, matrix]).astype(ml_dtypes.bfloat16)


def params(mib):
    return pltpu.CompilerParams(vmem_limit_bytes=mib * MIB)


def estimate(micros):
    return pl.CostEstimate(flops=int(micros * 1e9), bytes_accessed=int(micros * 1e6), transcendentals=0)


def scatter_levels(turned_ref, send_ref, fields, groups):
    size = groups * GROUP
    for field in range(fields):
        for group in range(groups):
            for level in range(SHARE):
                value = turned_ref[field * groups + group, pl.ds(level, WIDE, stride=SHARE), :]
                send_ref[pl.ds(group * GROUP + field * SHARE + level, WIDE, stride=size), :] = value


def pack_state(back_ref, traj_ref, pool_ref, send_ref, turned_ref, fine_ref):
    spare = jnp.zeros((8, 128), jnp.float32)
    fine_ref[...] = traj_ref[0].astype(jnp.float32).reshape(LEVELS * 64, 128)
    for group in range(4):
        for field in range(FIELDS):
            block = back_ref[field, 4 * group : 4 * group + 4].reshape(4 * COLS, LEVELS)
            turned_ref[field * 4 + group, 0:LEVELS, :] = block.T
            turned_ref[field * 4 + group, LEVELS:, :] = spare
        parts = []
        for part in range(4):
            first = 16 * group + 4 * part
            total = fine_ref[pl.ds(first, LEVELS, stride=64), :]
            for extra in range(1, 4):
                total = total + fine_ref[pl.ds(first + extra, LEVELS, stride=64), :]
            parts.append(total)
        mean = jnp.dot(
            jnp.concatenate(parts, axis=1),
            pool_ref[...],
            precision=lax.Precision.HIGHEST,
            preferred_element_type=jnp.float32,
        )
        turned_ref[FIELDS * 4 + group, 0:LEVELS, :] = advection_scale * jnp.tanh(mean)
        turned_ref[FIELDS * 4 + group, LEVELS:, :] = spare
    scatter_levels(turned_ref, send_ref, FIELDS + 1, 4)


def pack_departures(innov_ref, weight_ref, before_ref, after_ref, send_ref, turned_ref):
    spare = jnp.zeros((8, 128), jnp.float32)
    for field in range(FIELDS + 1):
        source = innov_ref.at[field] if field < FIELDS else weight_ref
        for group in range(5):
            if group < 4:
                block = source[4 * group : 4 * group + 4].reshape(4 * COLS, LEVELS)
            else:
                block = jnp.concatenate([before_ref[field], after_ref[field]], axis=0).reshape(4 * COLS, LEVELS)
            turned_ref[field * 5 + group, 0:LEVELS, :] = block.T
            turned_ref[field * 5 + group, LEVELS:, :] = spare
    scatter_levels(turned_ref, send_ref, FIELDS + 1, 5)


def lane_block():
    return lax.broadcasted_iota(jnp.int32, (GROUP, 128), 1) // COLS


def turn(value, blocks):
    shift = (COLS * blocks) % 128
    return value if shift == 0 else pltpu.roll(value, shift, 1)


def unpack_rows(load, store):
    block = lane_block()
    for quarter in range(4):
        pieces = [load(4 * quarter + source) for source in range(4)]
        for row in range(4):
            value = turn(pieces[0], -row)
            for source in range(1, 4):
                value = jnp.where(block == source, turn(pieces[source], source - row), value)
            store(row, slice(128 * quarter, 128 * quarter + 128), value)


def split_store(ref, at, value):
    high = value.astype(jnp.bfloat16)
    low = (value - high.astype(jnp.float32)).astype(jnp.bfloat16)
    ref[at, 0:HALF] = high
    ref[at, HALF:CYCLE] = low


def fold_store(even_ref, odd_ref, index, value):
    at = pl.ds(pl.multiple_of(index * GROUP, GROUP), GROUP)
    split_store(even_ref, at, value[:, :HALF] + value[:, HALF:])
    split_store(odd_ref, at, value[:, :HALF] - value[:, HALF:])


def product(ref, count, basis_ref, which):
    rows = slice(0, count)
    total = jnp.dot(ref[rows, :], basis_ref[which, 0:CYCLE], preferred_element_type=jnp.float32)
    return total + jnp.dot(
        ref[rows, 0:HALF], basis_ref[which, CYCLE:], preferred_element_type=jnp.float32
    )


def filtered(even_ref, odd_ref, basis_ref, resp_ref, first, rows, out_ref):
    count = rows * GROUP
    band = slice(first, first + rows)
    for ref, which, lanes in ((even_ref, 0, slice(0, HALF)), (odd_ref, 1, slice(HALF, CYCLE))):
        coefs = product(ref, count, basis_ref, which).reshape(rows, GROUP, HALF)
        coefs = (coefs * resp_ref[band, :, lanes]).reshape(count, HALF)
        split_store(ref, slice(0, count), coefs)
    even = product(even_ref, count, basis_ref, 2)
    odd = product(odd_ref, count, basis_ref, 3)
    out_ref[band, :, 0:HALF] = (even + odd).reshape(rows, GROUP, HALF)
    out_ref[band, :, HALF:CYCLE] = (even - odd).reshape(rows, GROUP, HALF)


def expand(source_ref, rows, out_ref):
    for field in range(FIELDS):
        out_ref[0:rows, SHARE * field : SHARE * field + SHARE, :] = source_ref[0:rows, PLANES : PLANES + SHARE, :]


def tangent(recv_ref, before_ref, after_ref, resp_ref, basis_ref, state_ref, drift_ref, row_ref, even_ref, odd_ref):
    for group in range(6):
        def load(source):
            if group == 0:
                return before_ref[source]
            if group == 5:
                return after_ref[source]
            return recv_ref[source, GROUP * (group - 1) : GROUP * group, :]

        def store(row, lanes, value):
            row_ref[4 * group + row, :, lanes] = value

        unpack_rows(load, store)
    drift_ref[:, GROUP - 8 :, :] = jnp.zeros((BAND, 8, CYCLE), jnp.float32)
    expand(row_ref, BAND, drift_ref)

    for step in range(2):
        first, last = 1 + step, BAND - 1 - step
        source_ref = row_ref if step == 0 else state_ref

        def body(index, carry):
            here = source_ref[index]
            east = pltpu.roll(here, CYCLE - 1, 1)
            west = pltpu.roll(here, 1, 1)
            near = source_ref[index - 1] + source_ref[index + 1] + east + west
            moved = here + diffusion * (near - 4.0 * here) + drift_ref[index] * (east - west)
            fold_store(even_ref, odd_ref, index - first, moved)
            return carry

        lax.fori_loop(first, last, body, 0)
        filtered(even_ref, odd_ref, basis_ref, resp_ref, first, last - first, state_ref)


def adjoint(recv_ref, state_ref, drift_ref, resp_ref, basis_ref, send_ref, row_ref, field_ref, weight_ref, even_ref, odd_ref):
    for group in range(5):
        def load(source):
            return recv_ref[source, GROUP * group : GROUP * group + GROUP, :]

        def store(row, lanes, value):
            if group < 4:
                at = 4 * group + row + HALO
            else:
                at = 2 + row if row < 2 else 18 + row
            row_ref[at, :, lanes] = value

        unpack_rows(load, store)
    weight_ref[:, GROUP - 8 :, :] = jnp.zeros((BAND, 8, CYCLE), jnp.float32)
    for field in range(FIELDS):
        weight_ref[2:22, SHARE * field : SHARE * field + SHARE, :] = row_ref[2:22, PLANES : PLANES + SHARE, :]

    def depart(index, carry):
        fold_store(even_ref, odd_ref, index - 2, weight_ref[index] * (state_ref[index] - row_ref[index]))
        return carry

    lax.fori_loop(2, 22, depart, 0)
    for step in range(2):
        first, last = 2 + step, BAND - 2 - step
        filtered(even_ref, odd_ref, basis_ref, resp_ref, first, last - first, field_ref)

        def body(index, carry):
            here = field_ref[index]
            carried = drift_ref[index] * here
            near = field_ref[index - 1] + field_ref[index + 1]
            near = near + pltpu.roll(here, CYCLE - 1, 1) + pltpu.roll(here, 1, 1)
            moved = here + diffusion * (near - 4.0 * here)
            moved = moved + pltpu.roll(carried, 1, 1) - pltpu.roll(carried, CYCLE - 1, 1)
            if step == 0:
                fold_store(even_ref, odd_ref, index - 3, moved)
            else:
                row_ref[index] = moved
            return carry

        lax.fori_loop(first + 1, last - 1, body, 0)
    block = lane_block()
    for group in range(4):
        for quarter in range(4):
            lanes = slice(128 * quarter, 128 * quarter + 128)
            pieces = [row_ref[HALO + 4 * group + row, :, lanes] for row in range(4)]
            for source in range(4):
                value = turn(pieces[0], -source)
                for row in range(1, 4):
                    value = jnp.where(block == row, turn(pieces[row], row - source), value)
                send_ref[4 * quarter + source, PLANES * group : PLANES * group + PLANES, :] = value[:PLANES]


def prolong(back_ref, cost_ref, traj_ref, spread_ref, out_ref, wide_ref):
    for group in range(4):
        change = (
            back_ref[0, GROUP * group : GROUP * group + PLANES, :]
            - cost_ref[0, PLANES * group : PLANES * group + PLANES, :]
        )
        high = change.astype(jnp.bfloat16)
        low = (change - high.astype(jnp.float32)).astype(jnp.bfloat16)
        spread = jnp.dot(
            jnp.concatenate([high, low], axis=1), spread_ref[...], preferred_element_type=jnp.float32
        )
        for part in range(4):
            wide_ref[4 * group + part, 0:PLANES, :] = spread[:, 128 * part : 128 * part + 128]
    upper = lax.broadcasted_iota(jnp.int32, (8, 128), 0) < 4
    for field in range(FIELDS):
        for level in range(SHARE):
            plane = field * SHARE + level
            rows = []
            for pair in range(8):
                above = jnp.broadcast_to(wide_ref[2 * pair, plane : plane + 1, :], (8, 128))
                below = jnp.broadcast_to(wide_ref[2 * pair + 1, plane : plane + 1, :], (8, 128))
                rows.append(jnp.where(upper, above, below))
            fine = jnp.concatenate(rows, axis=0)
            out_ref[field, level] = (traj_ref[field, level].astype(jnp.float32) + fine).astype(jnp.bfloat16)


def response_rows(narrow_index):
    row = narrow_index * ROWS - HALO + jnp.arange(BAND, dtype=jnp.int32)
    latitude = jnp.pi * ((row.astype(jnp.float32) + 0.5) / TOTAL_ROWS - 0.5)
    cutoff = 0.5 * CYCLE * jnp.cos(latitude)
    inside = (row >= 0) & (row < TOTAL_ROWS)
    cutoff = jnp.where(inside, cutoff, 1.0)
    scaled = jnp.asarray(WAVES, jnp.float32)[None, :] / cutoff[:, None]
    response = jnp.where(inside[:, None], 1.0 / (1.0 + scaled**4), 0.0)
    return response.reshape(BAND, 1, CYCLE)


def shards(trajectory, innovation, background, obs_weight):
    f32 = jnp.float32
    narrow_count = lax.axis_size("narrow")
    narrow_index = lax.axis_index("narrow")
    onward = [(i, i + 1) for i in range(narrow_count - 1)]
    backward = [(i + 1, i) for i in range(narrow_count - 1)]
    innov = innovation.transpose(0, 2, 3, 1)
    back = background.transpose(0, 2, 3, 1)
    weight = obs_weight.transpose(1, 2, 0)
    basis = jnp.asarray(BASIS)
    response = response_rows(narrow_index)

    def edge(rows):
        return jnp.concatenate([innov[:, rows], weight[None, rows]], axis=0)

    before = lax.ppermute(edge(slice(14, 16)), "narrow", onward)
    after = lax.ppermute(edge(slice(0, 2)), "narrow", backward)

    full = pl.BlockSpec(memory_space=pltpu.VMEM)
    send_state = pl.pallas_call(
        pack_state,
        grid=(1,),
        in_specs=[
            pl.BlockSpec((FIELDS, ROWS, COLS, LEVELS), lambda i: (0, 0, 0, 0)),
            pl.BlockSpec((1, LEVELS, 64, 128), lambda i: (0, 0, 0, 0)),
            pl.BlockSpec((512, 128), lambda i: (0, 0)),
        ],
        out_specs=pl.BlockSpec((WIDE * 4 * GROUP, 128), lambda i: (0, 0)),
        out_shape=jax.ShapeDtypeStruct((WIDE * 4 * GROUP, 128), f32),
        scratch_shapes=[pltpu.VMEM((24, 80, 128), f32), pltpu.VMEM((LEVELS * 64, 128), f32)],
        compiler_params=params(40),
        cost_estimate=estimate(3),
    )(back, trajectory, jnp.asarray(pooling()))
    send_state = send_state.reshape(WIDE, 4 * GROUP, 128)
    held_state = lax.all_to_all(send_state, "wide", split_axis=0, concat_axis=0, tiled=True)

    send_depart = pl.pallas_call(
        pack_departures,
        in_specs=[full] * 4,
        out_specs=full,
        out_shape=jax.ShapeDtypeStruct((WIDE * 5 * GROUP, 128), f32),
        scratch_shapes=[pltpu.VMEM((30, 80, 128), f32)],
        compiler_params=params(40),
        cost_estimate=estimate(3),
    )(innov, weight, before, after)
    send_depart = send_depart.reshape(WIDE, 5 * GROUP, 128)

    north = lax.ppermute(held_state[:, 3 * GROUP :], "narrow", onward)
    south = lax.ppermute(held_state[:, :GROUP], "narrow", backward)
    held_depart = lax.all_to_all(send_depart, "wide", split_axis=0, concat_axis=0, tiled=True)

    rows_shape = (BAND, GROUP, CYCLE)
    folded = pltpu.VMEM(((BAND - 2) * GROUP, CYCLE), jnp.bfloat16)
    state, drift = pl.pallas_call(
        tangent,
        in_specs=[full] * 5,
        out_specs=[full] * 2,
        out_shape=[jax.ShapeDtypeStruct(rows_shape, f32)] * 2,
        scratch_shapes=[pltpu.VMEM(rows_shape, f32), folded, folded],
        compiler_params=params(48),
        cost_estimate=estimate(5),
    )(held_state, north, south, response, basis)
    send_cost = pl.pallas_call(
        adjoint,
        in_specs=[full] * 5,
        out_specs=full,
        out_shape=jax.ShapeDtypeStruct((WIDE, 4 * PLANES, 128), f32),
        scratch_shapes=[pltpu.VMEM(rows_shape, f32)] * 3 + [folded, folded],
        compiler_params=params(48),
        cost_estimate=estimate(5),
    )(held_depart, state, drift, response, basis)
    costate = lax.all_to_all(send_cost, "wide", split_axis=0, concat_axis=0, tiled=True)

    fine_block = pl.BlockSpec((FIELDS, SHARE, 64, 128), lambda i: (0, i, 0, 0))
    return pl.pallas_call(
        prolong,
        grid=(pl.cdiv(LEVELS, SHARE),),
        in_specs=[
            pl.BlockSpec((1, 4 * GROUP, 128), lambda i: (i, 0, 0)),
            pl.BlockSpec((1, 4 * PLANES, 128), lambda i: (i, 0, 0)),
            fine_block,
            pl.BlockSpec((256, 512), lambda i: (0, 0)),
        ],
        out_specs=fine_block,
        out_shape=jax.ShapeDtypeStruct(trajectory.shape, jnp.bfloat16),
        scratch_shapes=[pltpu.VMEM((16, GROUP, 128), f32)],
        compiler_params=params(32),
        cost_estimate=estimate(5),
    )(send_state, costate, trajectory, jnp.asarray(spreading()))


def solution(mesh):
    in_specs = (
        P(None, None, "narrow", "wide"),
        P(None, None, "narrow", "wide"),
        P(None, None, "narrow", "wide"),
        P(None, "narrow", "wide"),
    )
    out_specs = P(None, None, "narrow", "wide")
    return jax.shard_map(shards, mesh=mesh, in_specs=in_specs, out_specs=out_specs, check_vma=False)
```

```python
import jax
import jax.numpy as jnp
import ml_dtypes
import numpy as np
from jax import lax
from jax.experimental import pallas as pl
from jax.experimental.pallas import tpu as pltpu
from jax.sharding import PartitionSpec as P

FIELDS = 5
LEVELS = 72
COARSEN = 4
ROWS = 16
COLS = 32
CYCLE = 512
HALF = 256
TOTAL_ROWS = 128
SHARE = 5
GROUP = 32
PLANES = FIELDS * SHARE
WIDE = 16
HALO = 4
BAND = ROWS + 2 * HALO
SLOTS = 3
KEPT = 448

diffusion = 0.2
advection_scale = 0.3
MIB = 2**20


def harmonics():
    column = np.arange(HALF)

    def wave(function, wavenumbers):
        angle = 2 * np.pi * ((column[:, None] * wavenumbers[None, :]) % CYCLE) / CYCLE
        scale = np.where((wavenumbers == 0) | (wavenumbers == HALF), 1.0, 2.0)
        return function(angle) * np.sqrt(scale / CYCLE)

    even_cos, even_sin = np.arange(0, HALF + 1, 2), np.arange(2, HALF, 2)
    odd = np.arange(1, HALF, 2)
    even = np.concatenate([wave(np.cos, even_cos), wave(np.sin, even_sin)], axis=1)
    odds = np.concatenate([wave(np.cos, odd), wave(np.sin, odd)], axis=1)
    order = np.concatenate([even_cos, even_sin, odd, odd])
    return even, odds, order


def stacked(matrix):
    high = matrix.astype(ml_dtypes.bfloat16)
    low = (matrix - high.astype(np.float64)).astype(ml_dtypes.bfloat16)
    return np.concatenate([high, low], axis=0)


EVEN, ODD, WAVES = harmonics()
BASIS = np.stack([stacked(EVEN), stacked(ODD), stacked(EVEN.T), stacked(ODD.T)])


def spreading():
    fine = np.arange(4 * COLS)
    matrix = np.zeros((4 * COLS, 4, 4 * COLS), np.float32)
    for part in range(4):
        matrix[part * COLS + fine // 4, part, fine] = 1.0
    matrix = matrix.reshape(4 * COLS, 16 * COLS)
    return np.concatenate([matrix, matrix]).astype(ml_dtypes.bfloat16)


def params(mib):
    return pltpu.CompilerParams(vmem_limit_bytes=mib * MIB)


def estimate(micros):
    return pl.CostEstimate(flops=int(micros * 1e9), bytes_accessed=int(micros * 1e6), transcendentals=0)


def scatter_levels(turned_ref, send_ref, fields, groups):
    size = groups * GROUP
    for field in range(fields):
        for group in range(groups):
            for level in range(SHARE):
                value = turned_ref[field * groups + group, pl.ds(level, WIDE, stride=SHARE), :]
                send_ref[pl.ds(group * GROUP + field * SHARE + level, WIDE, stride=size), :] = value


def pooling():
    fine = lax.broadcasted_iota(jnp.int32, (16 * COLS, 4 * COLS), 0)
    lane = lax.broadcasted_iota(jnp.int32, (16 * COLS, 4 * COLS), 1)
    meets = (fine // (4 * COLS) == lane // COLS) & ((fine % (4 * COLS)) // 4 == lane % COLS)
    return jnp.where(meets, 1.0 / 16, 0.0)


def pack_state(back_in, traj_in, send_ref, turned_ref, fine_ref, back_ref, wind_ref, sems):
    copies = [pltpu.make_async_copy(traj_in.at[0], wind_ref, sems.at[FIELDS])]
    copies += [pltpu.make_async_copy(back_in.at[f], back_ref.at[f], sems.at[f]) for f in range(FIELDS)]
    for copy in copies:
        copy.start()
    spare = jnp.zeros((8, 128), jnp.float32)
    pool = pooling()
    copies[0].wait()
    fine_ref[...] = wind_ref[...].astype(jnp.float32).reshape(LEVELS * 64, 128)
    for group in range(4):
        for field in range(FIELDS):
            if group == 0:
                copies[1 + field].wait()
            block = back_ref[field, 4 * group : 4 * group + 4].reshape(4 * COLS, LEVELS)
            turned_ref[field * 4 + group, 0:LEVELS, :] = block.T
            turned_ref[field * 4 + group, LEVELS:, :] = spare
        parts = []
        for part in range(4):
            first = 16 * group + 4 * part
            total = fine_ref[pl.ds(first, LEVELS, stride=64), :]
            for extra in range(1, 4):
                total = total + fine_ref[pl.ds(first + extra, LEVELS, stride=64), :]
            parts.append(total)
        mean = jnp.dot(
            jnp.concatenate(parts, axis=1),
            pool,
            precision=lax.Precision.HIGHEST,
            preferred_element_type=jnp.float32,
        )
        turned_ref[FIELDS * 4 + group, 0:LEVELS, :] = advection_scale * jnp.tanh(mean)
        turned_ref[FIELDS * 4 + group, LEVELS:, :] = spare
    scatter_levels(turned_ref, send_ref, FIELDS + 1, 4)


def pack_departures(innov_ref, weight_ref, before_ref, after_ref, send_ref, turned_ref):
    spare = jnp.zeros((8, 128), jnp.float32)
    for field in range(FIELDS + 1):
        source = innov_ref.at[field] if field < FIELDS else weight_ref
        for group in range(5):
            if group < 4:
                block = source[4 * group : 4 * group + 4].reshape(4 * COLS, LEVELS)
            else:
                block = jnp.concatenate([before_ref[field], after_ref[field]], axis=0).reshape(4 * COLS, LEVELS)
            turned_ref[field * 5 + group, 0:LEVELS, :] = block.T
            turned_ref[field * 5 + group, LEVELS:, :] = spare
    scatter_levels(turned_ref, send_ref, FIELDS + 1, 5)


def lane_block():
    return lax.broadcasted_iota(jnp.int32, (GROUP, 128), 1) // COLS


def turn(value, blocks):
    shift = (COLS * blocks) % 128
    return value if shift == 0 else pltpu.roll(value, shift, 1)


def unpack_rows(load, store):
    block = lane_block()
    for quarter in range(4):
        pieces = [load(4 * quarter + source) for source in range(4)]
        for row in range(4):
            value = turn(pieces[0], -row)
            for source in range(1, 4):
                value = jnp.where(block == source, turn(pieces[source], source - row), value)
            store(row, slice(128 * quarter, 128 * quarter + 128), value)


def split_store(ref, at, value):
    high = value.astype(jnp.bfloat16)
    low = (value - high.astype(jnp.float32)).astype(jnp.bfloat16)
    ref[at, 0:HALF] = high
    ref[at, HALF:CYCLE] = low


def fold_store(even_ref, odd_ref, index, value):
    at = pl.ds(pl.multiple_of(index * GROUP, GROUP), GROUP)
    split_store(even_ref, at, value[:, :HALF] + value[:, HALF:])
    split_store(odd_ref, at, value[:, :HALF] - value[:, HALF:])


def product(ref, count, basis_ref, which):
    high, low = ref[0:count, 0:HALF], ref[0:count, HALF:CYCLE]
    basis_high, basis_low = basis_ref[which, 0:HALF], basis_ref[which, HALF:CYCLE]
    total = jnp.dot(high, basis_high, preferred_element_type=jnp.float32)
    total = total + jnp.dot(low, basis_high, preferred_element_type=jnp.float32)
    return total + jnp.dot(high, basis_low, preferred_element_type=jnp.float32)


def filtered(even_ref, odd_ref, basis_ref, resp_ref, first, rows, out_ref):
    count = rows * GROUP
    band = slice(first, first + rows)
    for ref, which, lanes in ((even_ref, 0, slice(0, HALF)), (odd_ref, 1, slice(HALF, CYCLE))):
        coefs = product(ref, count, basis_ref, which).reshape(rows, GROUP, HALF)
        coefs = (coefs * resp_ref[band, :, lanes]).reshape(count, HALF)
        split_store(ref, slice(0, count), coefs)
    even = product(even_ref, count, basis_ref, 2)
    odd = product(odd_ref, count, basis_ref, 3)
    out_ref[band, :, 0:HALF] = (even + odd).reshape(rows, GROUP, HALF)
    out_ref[band, :, HALF:CYCLE] = (even - odd).reshape(rows, GROUP, HALF)


def expand(source_ref, rows, out_ref):
    for field in range(FIELDS):
        out_ref[0:rows, SHARE * field : SHARE * field + SHARE, :] = source_ref[0:rows, PLANES : PLANES + SHARE, :]


def tangent(recv_ref, before_ref, after_ref, resp_ref, basis_ref, kept_out, row_ref, state_ref, drift_ref, even_ref, odd_ref, sems):
    for group in range(6):
        def load(source):
            if group == 0:
                return before_ref[source]
            if group == 5:
                return after_ref[source]
            return recv_ref[source, GROUP * (group - 1) : GROUP * group, :]

        def store(row, lanes, value):
            row_ref[4 * group + row, :, lanes] = value

        unpack_rows(load, store)
    drift_ref[:, GROUP - 8 :, :] = jnp.zeros((BAND, 8, CYCLE), jnp.float32)
    expand(row_ref, BAND, drift_ref)
    drift_copy = pltpu.make_async_copy(drift_ref, kept_out.at[BAND : 2 * BAND], sems.at[0])
    drift_copy.start()

    for step in range(2):
        first, last = 1 + step, BAND - 1 - step
        source_ref = row_ref if step == 0 else state_ref

        def body(index, carry):
            here = source_ref[index]
            east = pltpu.roll(here, CYCLE - 1, 1)
            west = pltpu.roll(here, 1, 1)
            near = source_ref[index - 1] + source_ref[index + 1] + east + west
            moved = here + diffusion * (near - 4.0 * here) + drift_ref[index] * (east - west)
            fold_store(even_ref, odd_ref, index - first, moved)
            return carry

        lax.fori_loop(first, last, body, 0, unroll=4)
        filtered(even_ref, odd_ref, basis_ref, resp_ref, first, last - first, state_ref)
    state_copy = pltpu.make_async_copy(state_ref, kept_out.at[0:BAND], sems.at[1])
    state_copy.start()
    drift_copy.wait()
    state_copy.wait()


def adjoint(recv_ref, kept_in, traj_in, resp_ref, basis_ref, send_ref, held_ref, row_ref, field_ref, weight_ref, state_ref, drift_ref, even_ref, odd_ref, sems):
    held_copy = pltpu.make_async_copy(traj_in, held_ref, sems.at[2])
    state_copy = pltpu.make_async_copy(kept_in.at[0:BAND], state_ref, sems.at[0])
    state_copy.start()
    drift_copy = pltpu.make_async_copy(kept_in.at[BAND : 2 * BAND], drift_ref, sems.at[1])
    drift_copy.start()
    held_copy.start()
    for group in range(5):
        def load(source):
            return recv_ref[source, GROUP * group : GROUP * group + GROUP, :]

        def store(row, lanes, value):
            if group < 4:
                at = 4 * group + row + HALO
            else:
                at = 2 + row if row < 2 else 18 + row
            row_ref[at, :, lanes] = value

        unpack_rows(load, store)
    weight_ref[:, GROUP - 8 :, :] = jnp.zeros((BAND, 8, CYCLE), jnp.float32)
    for field in range(FIELDS):
        weight_ref[2:22, SHARE * field : SHARE * field + SHARE, :] = row_ref[2:22, PLANES : PLANES + SHARE, :]

    state_copy.wait()
    drift_copy.wait()

    def depart(index, carry):
        fold_store(even_ref, odd_ref, index - 2, weight_ref[index] * (state_ref[index] - row_ref[index]))
        return carry

    lax.fori_loop(2, 22, depart, 0, unroll=4)
    for step in range(2):
        first, last = 2 + step, BAND - 2 - step
        filtered(even_ref, odd_ref, basis_ref, resp_ref, first, last - first, field_ref)

        def body(index, carry):
            here = field_ref[index]
            carried = drift_ref[index] * here
            near = field_ref[index - 1] + field_ref[index + 1]
            near = near + pltpu.roll(here, CYCLE - 1, 1) + pltpu.roll(here, 1, 1)
            moved = here + diffusion * (near - 4.0 * here)
            moved = moved + pltpu.roll(carried, 1, 1) - pltpu.roll(carried, CYCLE - 1, 1)
            if step == 0:
                fold_store(even_ref, odd_ref, index - 3, moved)
            else:
                row_ref[index] = moved
            return carry

        lax.fori_loop(first + 1, last - 1, body, 0, unroll=4)
    block = lane_block()
    for group in range(4):
        for quarter in range(4):
            lanes = slice(128 * quarter, 128 * quarter + 128)
            pieces = [row_ref[HALO + 4 * group + row, :, lanes] for row in range(4)]
            for source in range(4):
                value = turn(pieces[0], -source)
                for row in range(1, 4):
                    value = jnp.where(block == row, turn(pieces[row], row - source), value)
                send_ref[4 * quarter + source, PLANES * group : PLANES * group + PLANES, :] = value[:PLANES]
    held_copy.wait()


def prolong(back_ref, cost_ref, traj_ref, spread_ref, out_ref, wide_ref, slot_ref, sems):
    whole, rest = LEVELS // SHARE, LEVELS % SHARE

    upper = lax.broadcasted_iota(jnp.int32, (8, 128), 0) < 4

    def fill(owner, slot, levels):
        for group in range(4):
            change = (
                back_ref[owner, GROUP * group : GROUP * group + PLANES, :]
                - cost_ref[owner, PLANES * group : PLANES * group + PLANES, :]
            )
            high = change.astype(jnp.bfloat16)
            low = (change - high.astype(jnp.float32)).astype(jnp.bfloat16)
            spread = jnp.dot(
                jnp.concatenate([high, low], axis=1), spread_ref[...], preferred_element_type=jnp.float32
            )
            for part in range(4):
                wide_ref[4 * group + part, 0:PLANES, :] = spread[:, 128 * part : 128 * part + 128]
        for field in range(FIELDS):
            for level in range(levels):
                plane = field * SHARE + level
                rows = []
                for pair in range(8):
                    above = jnp.broadcast_to(wide_ref[2 * pair, plane : plane + 1, :], (8, 128))
                    below = jnp.broadcast_to(wide_ref[2 * pair + 1, plane : plane + 1, :], (8, 128))
                    rows.append(jnp.where(upper, above, below))
                fine = jnp.concatenate(rows, axis=0)
                first_guess = traj_ref[field, SHARE * owner + level].astype(jnp.float32)
                slot_ref[slot, field, level] = (first_guess + fine).astype(jnp.bfloat16)

    def copy(owner, slot, levels=SHARE):
        return pltpu.make_async_copy(
            slot_ref.at[slot, :, 0:levels], out_ref.at[:, pl.ds(SHARE * owner, levels)], sems.at[slot]
        )

    for owner in range(SLOTS):
        fill(owner, owner, SHARE)
        copy(owner, owner).start()

    def body(owner, carry):
        slot = lax.rem(owner, SLOTS)
        copy(owner - SLOTS, slot).wait()
        fill(owner, slot, SHARE)
        copy(owner, slot).start()
        return carry

    lax.fori_loop(SLOTS, whole, body, 0)
    slot = whole % SLOTS
    copy(whole - SLOTS, slot).wait()
    fill(whole, slot, rest)
    copy(whole, slot, rest).start()
    for owner in range(whole - SLOTS + 1, whole):
        copy(owner, owner % SLOTS).wait()
    copy(whole, slot, rest).wait()


def response_rows(narrow_index):
    row = narrow_index * ROWS - HALO + jnp.arange(BAND, dtype=jnp.int32)
    latitude = jnp.pi * ((row.astype(jnp.float32) + 0.5) / TOTAL_ROWS - 0.5)
    cutoff = 0.5 * CYCLE * jnp.cos(latitude)
    inside = (row >= 0) & (row < TOTAL_ROWS)
    cutoff = jnp.where(inside, cutoff, 1.0)
    scaled = jnp.asarray(WAVES, jnp.float32)[None, :] / cutoff[:, None]
    response = jnp.where(inside[:, None], 1.0 / (1.0 + scaled**4), 0.0)
    return response.reshape(BAND, 1, CYCLE)


def shards(trajectory, innovation, background, obs_weight):
    f32 = jnp.float32
    narrow_count = lax.axis_size("narrow")
    narrow_index = lax.axis_index("narrow")
    onward = [(i, i + 1) for i in range(narrow_count - 1)]
    backward = [(i + 1, i) for i in range(narrow_count - 1)]
    innov = innovation.transpose(0, 2, 3, 1)
    back = background.transpose(0, 2, 3, 1)
    weight = obs_weight.transpose(1, 2, 0)
    basis = jnp.asarray(BASIS)
    response = response_rows(narrow_index)

    def edge(rows):
        return jnp.concatenate([innov[:, rows], weight[None, rows]], axis=0)

    before = lax.ppermute(edge(slice(14, 16)), "narrow", onward)
    after = lax.ppermute(edge(slice(0, 2)), "narrow", backward)

    full = pl.BlockSpec(memory_space=pltpu.VMEM)
    away = pl.BlockSpec(memory_space=pltpu.HBM)
    send_state = pl.pallas_call(
        pack_state,
        in_specs=[away] * 2,
        out_specs=full,
        out_shape=jax.ShapeDtypeStruct((WIDE * 4 * GROUP, 128), f32),
        scratch_shapes=[
            pltpu.VMEM((24, 80, 128), f32),
            pltpu.VMEM((LEVELS * 64, 128), f32),
            pltpu.VMEM((FIELDS, ROWS, COLS, LEVELS), f32),
            pltpu.VMEM((LEVELS, 64, 128), jnp.bfloat16),
            pltpu.SemaphoreType.DMA((FIELDS + 1,)),
        ],
        compiler_params=params(60),
        cost_estimate=estimate(3),
    )(back, trajectory)
    send_state = send_state.reshape(WIDE, 4 * GROUP, 128)
    held_state = lax.all_to_all(send_state, "wide", split_axis=0, concat_axis=0, tiled=True)

    send_depart = pl.pallas_call(
        pack_departures,
        in_specs=[full] * 4,
        out_specs=full,
        out_shape=jax.ShapeDtypeStruct((WIDE * 5 * GROUP, 128), f32),
        scratch_shapes=[pltpu.VMEM((30, 80, 128), f32)],
        compiler_params=params(16),
        cost_estimate=estimate(3),
    )(innov, weight, before, after)
    send_depart = send_depart.reshape(WIDE, 5 * GROUP, 128)

    north = lax.ppermute(held_state[:, 3 * GROUP :], "narrow", onward)
    south = lax.ppermute(held_state[:, :GROUP], "narrow", backward)
    held_depart = lax.all_to_all(send_depart, "wide", split_axis=0, concat_axis=0, tiled=True)

    rows_shape = (BAND, GROUP, CYCLE)
    folded = pltpu.VMEM(((BAND - 2) * GROUP, CYCLE), jnp.bfloat16)
    kept = pl.pallas_call(
        tangent,
        in_specs=[full] * 5,
        out_specs=away,
        out_shape=jax.ShapeDtypeStruct((KEPT, GROUP, CYCLE), f32),
        scratch_shapes=[pltpu.VMEM(rows_shape, f32)] * 3 + [folded, folded, pltpu.SemaphoreType.DMA((2,))],
        compiler_params=params(40),
        cost_estimate=estimate(5),
    )(held_state, north, south, response, basis)
    send_cost, held = pl.pallas_call(
        adjoint,
        in_specs=[full, away, away, full, full],
        out_specs=[full, full],
        out_shape=[
            jax.ShapeDtypeStruct((WIDE, 4 * PLANES, 128), f32),
            jax.ShapeDtypeStruct(trajectory.shape, jnp.bfloat16),
        ],
        scratch_shapes=[pltpu.VMEM(rows_shape, f32)] * 5 + [folded, folded, pltpu.SemaphoreType.DMA((3,))],
        compiler_params=params(40),
        cost_estimate=estimate(5),
    )(held_depart, kept, trajectory, response, basis)
    costate = lax.all_to_all(send_cost, "wide", split_axis=0, concat_axis=0, tiled=True)

    return pl.pallas_call(
        prolong,
        in_specs=[full] * 4,
        out_specs=away,
        out_shape=jax.ShapeDtypeStruct(trajectory.shape, jnp.bfloat16),
        scratch_shapes=[
            pltpu.VMEM((16, GROUP, 128), f32),
            pltpu.VMEM((SLOTS, FIELDS, SHARE, 64, 128), jnp.bfloat16),
            pltpu.SemaphoreType.DMA((SLOTS,)),
        ],
        compiler_params=params(24),
        cost_estimate=estimate(5),
    )(send_state, costate, held, jnp.asarray(spreading()))


def solution(mesh):
    in_specs = (
        P(None, None, "narrow", "wide"),
        P(None, None, "narrow", "wide"),
        P(None, None, "narrow", "wide"),
        P(None, "narrow", "wide"),
    )
    out_specs = P(None, None, "narrow", "wide")
    return jax.shard_map(shards, mesh=mesh, in_specs=in_specs, out_specs=out_specs, check_vma=False)
```

```python
import jax
import jax.numpy as jnp
import ml_dtypes
import numpy as np
from jax import lax
from jax.experimental import pallas as pl
from jax.experimental.pallas import tpu as pltpu
from jax.sharding import PartitionSpec as P

FIELDS = 5
LEVELS = 72
COARSEN = 4
ROWS = 16
COLS = 32
CYCLE = 512
HALF = 256
TOTAL_ROWS = 128
SHARE = 5
GROUP = 32
PLANES = FIELDS * SHARE
WIDE = 16
HALO = 4
BAND = ROWS + 2 * HALO
SLOTS = 3
KEPT = 448

diffusion = 0.2
advection_scale = 0.3
MIB = 2**20


def harmonics():
    column = np.arange(HALF)

    def wave(function, wavenumbers):
        angle = 2 * np.pi * ((column[:, None] * wavenumbers[None, :]) % CYCLE) / CYCLE
        scale = np.where((wavenumbers == 0) | (wavenumbers == HALF), 1.0, 2.0)
        return function(angle) * np.sqrt(scale / CYCLE)

    even_cos, even_sin = np.arange(0, HALF + 1, 2), np.arange(2, HALF, 2)
    odd = np.arange(1, HALF, 2)
    even = np.concatenate([wave(np.cos, even_cos), wave(np.sin, even_sin)], axis=1)
    odds = np.concatenate([wave(np.cos, odd), wave(np.sin, odd)], axis=1)
    order = np.concatenate([even_cos, even_sin, odd, odd])
    return even, odds, order


def stacked(matrix):
    high = matrix.astype(ml_dtypes.bfloat16)
    low = (matrix - high.astype(np.float64)).astype(ml_dtypes.bfloat16)
    return np.concatenate([high, low], axis=0)


EVEN, ODD, WAVES = harmonics()
BASIS = np.stack([stacked(EVEN), stacked(ODD), stacked(EVEN.T), stacked(ODD.T)])


def spreading():
    fine = np.arange(4 * COLS)
    matrix = np.zeros((4 * COLS, 4, 4 * COLS), np.float32)
    for part in range(4):
        matrix[part * COLS + fine // 4, part, fine] = 1.0
    matrix = matrix.reshape(4 * COLS, 16 * COLS)
    return np.concatenate([matrix, matrix]).astype(ml_dtypes.bfloat16)


def params(mib):
    return pltpu.CompilerParams(vmem_limit_bytes=mib * MIB)


def estimate(micros):
    return pl.CostEstimate(flops=int(micros * 1e9), bytes_accessed=int(micros * 1e6), transcendentals=0)


def scatter_levels(turned_ref, send_ref, fields, groups, flip):
    size = groups * GROUP
    for field in range(fields):
        for group in range(groups):
            for level in range(SHARE):
                for half in range(2):
                    first = half * SHARE * WIDE // 2 + level
                    value = turned_ref[field * groups + group, pl.ds(first, WIDE // 2, stride=SHARE), :]
                    owner = (WIDE // 2) * (half + flip - 2 * half * flip)
                    at = owner * size + group * GROUP + field * SHARE + level
                    send_ref[pl.ds(at, WIDE // 2, stride=size), :] = value


def pooling():
    fine = lax.broadcasted_iota(jnp.int32, (16 * COLS, 4 * COLS), 0)
    lane = lax.broadcasted_iota(jnp.int32, (16 * COLS, 4 * COLS), 1)
    meets = (fine // (4 * COLS) == lane // COLS) & ((fine % (4 * COLS)) // 4 == lane % COLS)
    return jnp.where(meets, 1.0 / 16, 0.0)


def pack_state(place_ref, back_in, traj_in, send_ref, turned_ref, fine_ref, back_ref, wind_ref, sems):
    copies = [pltpu.make_async_copy(traj_in.at[0], wind_ref, sems.at[FIELDS])]
    copies += [pltpu.make_async_copy(back_in.at[f], back_ref.at[f], sems.at[f]) for f in range(FIELDS)]
    for copy in copies:
        copy.start()
    spare = jnp.zeros((8, 128), jnp.float32)
    pool = pooling()
    copies[0].wait()
    fine_ref[...] = wind_ref[...].astype(jnp.float32).reshape(LEVELS * 64, 128)
    for group in range(4):
        for field in range(FIELDS):
            if group == 0:
                copies[1 + field].wait()
            block = back_ref[field, 4 * group : 4 * group + 4].reshape(4 * COLS, LEVELS)
            turned_ref[field * 4 + group, 0:LEVELS, :] = block.T
            turned_ref[field * 4 + group, LEVELS:, :] = spare
        parts = []
        for part in range(4):
            first = 16 * group + 4 * part
            total = fine_ref[pl.ds(first, LEVELS, stride=64), :]
            for extra in range(1, 4):
                total = total + fine_ref[pl.ds(first + extra, LEVELS, stride=64), :]
            parts.append(total)
        mean = jnp.dot(
            jnp.concatenate(parts, axis=1),
            pool,
            precision=lax.Precision.HIGHEST,
            preferred_element_type=jnp.float32,
        )
        turned_ref[FIELDS * 4 + group, 0:LEVELS, :] = advection_scale * jnp.tanh(mean)
        turned_ref[FIELDS * 4 + group, LEVELS:, :] = spare
    scatter_levels(turned_ref, send_ref, FIELDS + 1, 4, place_ref[0])


def pack_departures(place_ref, innov_ref, weight_ref, near_ref, far_ref, send_ref, turned_ref):
    spare = jnp.zeros((8, 128), jnp.float32)
    for field in range(FIELDS + 1):
        source = innov_ref.at[field] if field < FIELDS else weight_ref
        for group in range(5):
            if group < 4:
                block = source[4 * group : 4 * group + 4].reshape(4 * COLS, LEVELS)
            else:
                near, far = near_ref[field], far_ref[field]
                before = jnp.where(place_ref[3] == 1, near, far)
                after = jnp.where(place_ref[3] == 1, far, near)
                block = jnp.concatenate([before, after], axis=0).reshape(4 * COLS, LEVELS)
            turned_ref[field * 5 + group, 0:LEVELS, :] = block.T
            turned_ref[field * 5 + group, LEVELS:, :] = spare
    scatter_levels(turned_ref, send_ref, FIELDS + 1, 5, place_ref[0])


def lane_block():
    return lax.broadcasted_iota(jnp.int32, (GROUP, 128), 1) // COLS


def turn(value, blocks):
    shift = (COLS * blocks) % 128
    return value if shift == 0 else pltpu.roll(value, shift, 1)


def unpack_rows(load, store):
    block = lane_block()
    for quarter in range(4):
        pieces = [load(4 * quarter + source) for source in range(4)]
        for row in range(4):
            value = turn(pieces[0], -row)
            for source in range(1, 4):
                value = jnp.where(block == source, turn(pieces[source], source - row), value)
            store(row, quarter, value)


def split_store(ref, at, value):
    high = value.astype(jnp.bfloat16)
    low = (value - high.astype(jnp.float32)).astype(jnp.bfloat16)
    ref[at, 0:HALF] = high
    ref[at, HALF:CYCLE] = low


def fold_store(even_ref, odd_ref, index, value):
    at = pl.ds(pl.multiple_of(index * GROUP, GROUP), GROUP)
    split_store(even_ref, at, value[:, :HALF] + value[:, HALF:])
    split_store(odd_ref, at, value[:, :HALF] - value[:, HALF:])


def product(ref, count, basis_ref, which):
    high, low = ref[0:count, 0:HALF], ref[0:count, HALF:CYCLE]
    basis_high, basis_low = basis_ref[which, 0:HALF], basis_ref[which, HALF:CYCLE]
    total = jnp.dot(high, basis_high, preferred_element_type=jnp.float32)
    total = total + jnp.dot(low, basis_high, preferred_element_type=jnp.float32)
    return total + jnp.dot(high, basis_low, preferred_element_type=jnp.float32)


def filtered(even_ref, odd_ref, basis_ref, resp_ref, first, rows, out_ref):
    count = rows * GROUP
    band = slice(first, first + rows)
    for ref, which, lanes in ((even_ref, 0, slice(0, HALF)), (odd_ref, 1, slice(HALF, CYCLE))):
        coefs = product(ref, count, basis_ref, which).reshape(rows, GROUP, HALF)
        coefs = (coefs * resp_ref[band, :, lanes]).reshape(count, HALF)
        split_store(ref, slice(0, count), coefs)
    even = product(even_ref, count, basis_ref, 2)
    odd = product(odd_ref, count, basis_ref, 3)
    out_ref[band, :, 0:HALF] = (even + odd).reshape(rows, GROUP, HALF)
    out_ref[band, :, HALF:CYCLE] = (even - odd).reshape(rows, GROUP, HALF)


def expand(source_ref, rows, out_ref):
    for field in range(FIELDS):
        out_ref[0:rows, SHARE * field : SHARE * field + SHARE, :] = source_ref[0:rows, PLANES : PLANES + SHARE, :]


def tangent(place_ref, recv_ref, near_ref, far_ref, resp_ref, basis_ref, kept_out, row_ref, state_ref, drift_ref, even_ref, odd_ref, sems):
    for group in range(6):
        def load(source):
            if group == 0:
                return jnp.where(place_ref[3] == 1, near_ref[source], far_ref[source])
            if group == 5:
                return jnp.where(place_ref[3] == 1, far_ref[source], near_ref[source])
            return recv_ref[source, GROUP * (group - 1) : GROUP * group, :]

        def store(row, quarter, value):
            row_ref[4 * group + row, :, 128 * quarter : 128 * quarter + 128] = value

        unpack_rows(load, store)
    drift_ref[:, GROUP - 8 :, :] = jnp.zeros((BAND, 8, CYCLE), jnp.float32)
    expand(row_ref, BAND, drift_ref)
    drift_copy = pltpu.make_async_copy(drift_ref, kept_out.at[BAND : 2 * BAND], sems.at[0])
    drift_copy.start()

    for step in range(2):
        first, last = 1 + step, BAND - 1 - step
        source_ref = row_ref if step == 0 else state_ref

        def body(index, carry):
            here = source_ref[index]
            east = pltpu.roll(here, CYCLE - 1, 1)
            west = pltpu.roll(here, 1, 1)
            near = source_ref[index - 1] + source_ref[index + 1] + east + west
            moved = here + diffusion * (near - 4.0 * here) + drift_ref[index] * (east - west)
            fold_store(even_ref, odd_ref, index - first, moved)
            return carry

        lax.fori_loop(first, last, body, 0, unroll=4)
        filtered(even_ref, odd_ref, basis_ref, resp_ref, first, last - first, state_ref)
    state_copy = pltpu.make_async_copy(state_ref, kept_out.at[0:BAND], sems.at[1])
    state_copy.start()
    drift_copy.wait()
    state_copy.wait()


def adjoint(place_ref, recv_ref, kept_in, traj_in, resp_ref, basis_ref, send_ref, held_ref, row_ref, field_ref, weight_ref, state_ref, drift_ref, even_ref, odd_ref, sems):
    held_copy = pltpu.make_async_copy(traj_in, held_ref, sems.at[2])
    state_copy = pltpu.make_async_copy(kept_in.at[0:BAND], state_ref, sems.at[0])
    state_copy.start()
    drift_copy = pltpu.make_async_copy(kept_in.at[BAND : 2 * BAND], drift_ref, sems.at[1])
    drift_copy.start()
    held_copy.start()
    for group in range(5):
        def load(source):
            return recv_ref[source, GROUP * group : GROUP * group + GROUP, :]

        def store(row, quarter, value):
            if group < 4:
                row_ref[4 * group + row + HALO, :, 128 * quarter : 128 * quarter + 128] = value
            else:
                at = 2 + row if row < 2 else 18 + row
                swapped = place_ref[1] if row < 2 else place_ref[2]
                lanes = pl.multiple_of(128 * lax.rem(quarter + 2 * swapped, 4), 128)
                row_ref[at, :, pl.ds(lanes, 128)] = value

        unpack_rows(load, store)
    weight_ref[:, GROUP - 8 :, :] = jnp.zeros((BAND, 8, CYCLE), jnp.float32)
    for field in range(FIELDS):
        weight_ref[2:22, SHARE * field : SHARE * field + SHARE, :] = row_ref[2:22, PLANES : PLANES + SHARE, :]

    state_copy.wait()
    drift_copy.wait()

    def depart(index, carry):
        fold_store(even_ref, odd_ref, index - 2, weight_ref[index] * (state_ref[index] - row_ref[index]))
        return carry

    lax.fori_loop(2, 22, depart, 0, unroll=4)
    for step in range(2):
        first, last = 2 + step, BAND - 2 - step
        filtered(even_ref, odd_ref, basis_ref, resp_ref, first, last - first, field_ref)

        def body(index, carry):
            here = field_ref[index]
            carried = drift_ref[index] * here
            near = field_ref[index - 1] + field_ref[index + 1]
            near = near + pltpu.roll(here, CYCLE - 1, 1) + pltpu.roll(here, 1, 1)
            moved = here + diffusion * (near - 4.0 * here)
            moved = moved + pltpu.roll(carried, 1, 1) - pltpu.roll(carried, CYCLE - 1, 1)
            if step == 0:
                fold_store(even_ref, odd_ref, index - 3, moved)
            else:
                row_ref[index] = moved
            return carry

        lax.fori_loop(first + 1, last - 1, body, 0, unroll=4)
    block = lane_block()
    for group in range(4):
        for quarter in range(4):
            lanes = slice(128 * quarter, 128 * quarter + 128)
            pieces = [row_ref[HALO + 4 * group + row, :, lanes] for row in range(4)]
            for source in range(4):
                value = turn(pieces[0], -source)
                for row in range(1, 4):
                    value = jnp.where(block == row, turn(pieces[row], row - source), value)
                send_ref[4 * quarter + source, PLANES * group : PLANES * group + PLANES, :] = value[:PLANES]
    held_copy.wait()


def prolong(place_ref, back_ref, cost_ref, traj_ref, spread_ref, out_ref, wide_ref, slot_ref, sems):
    whole, rest = LEVELS // SHARE, LEVELS % SHARE

    upper = lax.broadcasted_iota(jnp.int32, (8, 128), 0) < 4

    def fill(owner, slot, levels):
        source = lax.rem(owner + (WIDE // 2) * place_ref[0], WIDE)
        for group in range(4):
            change = (
                back_ref[source, GROUP * group : GROUP * group + PLANES, :]
                - cost_ref[source, PLANES * group : PLANES * group + PLANES, :]
            )
            high = change.astype(jnp.bfloat16)
            low = (change - high.astype(jnp.float32)).astype(jnp.bfloat16)
            spread = jnp.dot(
                jnp.concatenate([high, low], axis=1), spread_ref[...], preferred_element_type=jnp.float32
            )
            for part in range(4):
                wide_ref[4 * group + part, 0:PLANES, :] = spread[:, 128 * part : 128 * part + 128]
        for field in range(FIELDS):
            for level in range(levels):
                plane = field * SHARE + level
                rows = []
                for pair in range(8):
                    above = jnp.broadcast_to(wide_ref[2 * pair, plane : plane + 1, :], (8, 128))
                    below = jnp.broadcast_to(wide_ref[2 * pair + 1, plane : plane + 1, :], (8, 128))
                    rows.append(jnp.where(upper, above, below))
                fine = jnp.concatenate(rows, axis=0)
                first_guess = traj_ref[field, SHARE * owner + level].astype(jnp.float32)
                slot_ref[slot, field, level] = (first_guess + fine).astype(jnp.bfloat16)

    def copy(owner, slot, levels=SHARE):
        return pltpu.make_async_copy(
            slot_ref.at[slot, :, 0:levels], out_ref.at[:, pl.ds(SHARE * owner, levels)], sems.at[slot]
        )

    for owner in range(SLOTS):
        fill(owner, owner, SHARE)
        copy(owner, owner).start()

    def body(owner, carry):
        slot = lax.rem(owner, SLOTS)
        copy(owner - SLOTS, slot).wait()
        fill(owner, slot, SHARE)
        copy(owner, slot).start()
        return carry

    lax.fori_loop(SLOTS, whole, body, 0)
    slot = whole % SLOTS
    copy(whole - SLOTS, slot).wait()
    fill(whole, slot, rest)
    copy(whole, slot, rest).start()
    for owner in range(whole - SLOTS + 1, whole):
        copy(owner, owner % SLOTS).wait()
    copy(whole, slot, rest).wait()


def response_rows(narrow_index):
    row = narrow_index * ROWS - HALO + jnp.arange(BAND, dtype=jnp.int32)
    latitude = jnp.pi * ((row.astype(jnp.float32) + 0.5) / TOTAL_ROWS - 0.5)
    cutoff = 0.5 * CYCLE * jnp.cos(latitude)
    inside = (row >= 0) & (row < TOTAL_ROWS)
    cutoff = jnp.where(inside, cutoff, 1.0)
    scaled = jnp.asarray(WAVES, jnp.float32)[None, :] / cutoff[:, None]
    response = jnp.where(inside[:, None], 1.0 / (1.0 + scaled**4), 0.0)
    return response.reshape(BAND, 1, CYCLE)


def shards(trajectory, innovation, background, obs_weight):
    f32 = jnp.float32
    narrow_count = lax.axis_size("narrow")
    narrow_index = lax.axis_index("narrow")
    middle = narrow_count // 2
    near, far = [], []
    for row in range(narrow_count - 1):
        for lane in range(WIDE):
            other = (lane + WIDE // 2) % WIDE if row == middle - 1 else lane
            one, two = lane * narrow_count + row, other * narrow_count + row + 1
            swaps = near if row % 2 == 0 else far
            swaps += [(one, two), (two, one)]
    odd = narrow_index % 2 == 1
    place = jnp.stack([narrow_index >= middle, narrow_index == middle, narrow_index == middle - 1, odd]).astype(jnp.int32)
    innov = innovation.transpose(0, 2, 3, 1)
    back = background.transpose(0, 2, 3, 1)
    weight = obs_weight.transpose(1, 2, 0)
    basis = jnp.asarray(BASIS)
    response = response_rows(narrow_index)

    def edge(rows):
        return jnp.concatenate([innov[:, rows], weight[None, rows]], axis=0)

    first, last = edge(slice(0, 2)), edge(slice(14, 16))
    edge_near = lax.ppermute(jnp.where(odd, first, last), ("wide", "narrow"), near)
    edge_far = lax.ppermute(jnp.where(odd, last, first), ("wide", "narrow"), far)

    full = pl.BlockSpec(memory_space=pltpu.VMEM)
    away = pl.BlockSpec(memory_space=pltpu.HBM)
    small = pl.BlockSpec(memory_space=pltpu.SMEM)
    send_state = pl.pallas_call(
        pack_state,
        in_specs=[small, away, away],
        out_specs=full,
        out_shape=jax.ShapeDtypeStruct((WIDE * 4 * GROUP, 128), f32),
        scratch_shapes=[
            pltpu.VMEM((24, 80, 128), f32),
            pltpu.VMEM((LEVELS * 64, 128), f32),
            pltpu.VMEM((FIELDS, ROWS, COLS, LEVELS), f32),
            pltpu.VMEM((LEVELS, 64, 128), jnp.bfloat16),
            pltpu.SemaphoreType.DMA((FIELDS + 1,)),
        ],
        compiler_params=params(60),
        cost_estimate=estimate(3),
    )(place, back, trajectory)
    send_state = send_state.reshape(WIDE, 4 * GROUP, 128)
    held_state = lax.all_to_all(send_state, "wide", split_axis=0, concat_axis=0, tiled=True)

    send_depart = pl.pallas_call(
        pack_departures,
        in_specs=[small] + [full] * 4,
        out_specs=full,
        out_shape=jax.ShapeDtypeStruct((WIDE * 5 * GROUP, 128), f32),
        scratch_shapes=[pltpu.VMEM((30, 80, 128), f32)],
        compiler_params=params(16),
        cost_estimate=estimate(3),
    )(place, innov, weight, edge_near, edge_far)
    send_depart = send_depart.reshape(WIDE, 5 * GROUP, 128)

    first, last = held_state[:, :GROUP], held_state[:, 3 * GROUP :]
    rows_near = lax.ppermute(jnp.where(odd, first, last), ("wide", "narrow"), near)
    rows_far = lax.ppermute(jnp.where(odd, last, first), ("wide", "narrow"), far)
    held_depart = lax.all_to_all(send_depart, "wide", split_axis=0, concat_axis=0, tiled=True)

    rows_shape = (BAND, GROUP, CYCLE)
    folded = pltpu.VMEM(((BAND - 2) * GROUP, CYCLE), jnp.bfloat16)
    kept = pl.pallas_call(
        tangent,
        in_specs=[small] + [full] * 5,
        out_specs=away,
        out_shape=jax.ShapeDtypeStruct((KEPT, GROUP, CYCLE), f32),
        scratch_shapes=[pltpu.VMEM(rows_shape, f32)] * 3 + [folded, folded, pltpu.SemaphoreType.DMA((2,))],
        compiler_params=params(40),
        cost_estimate=estimate(5),
    )(place, held_state, rows_near, rows_far, response, basis)
    send_cost, held = pl.pallas_call(
        adjoint,
        in_specs=[small, full, away, away, full, full],
        out_specs=[full, full],
        out_shape=[
            jax.ShapeDtypeStruct((WIDE, 4 * PLANES, 128), f32),
            jax.ShapeDtypeStruct(trajectory.shape, jnp.bfloat16),
        ],
        scratch_shapes=[pltpu.VMEM(rows_shape, f32)] * 5 + [folded, folded, pltpu.SemaphoreType.DMA((3,))],
        compiler_params=params(40),
        cost_estimate=estimate(5),
    )(place, held_depart, kept, trajectory, response, basis)
    costate = lax.all_to_all(send_cost, "wide", split_axis=0, concat_axis=0, tiled=True)

    return pl.pallas_call(
        prolong,
        in_specs=[small] + [full] * 4,
        out_specs=away,
        out_shape=jax.ShapeDtypeStruct(trajectory.shape, jnp.bfloat16),
        scratch_shapes=[
            pltpu.VMEM((16, GROUP, 128), f32),
            pltpu.VMEM((SLOTS, FIELDS, SHARE, 64, 128), jnp.bfloat16),
            pltpu.SemaphoreType.DMA((SLOTS,)),
        ],
        compiler_params=params(24),
        cost_estimate=estimate(5),
    )(place, send_state, costate, held, jnp.asarray(spreading()))


def solution(mesh):
    in_specs = (
        P(None, None, "narrow", "wide"),
        P(None, None, "narrow", "wide"),
        P(None, None, "narrow", "wide"),
        P(None, "narrow", "wide"),
    )
    out_specs = P(None, None, "narrow", "wide")
    return jax.shard_map(shards, mesh=mesh, in_specs=in_specs, out_specs=out_specs, check_vma=False)
```

```python
import jax
import jax.numpy as jnp
import ml_dtypes
import numpy as np
from jax import lax
from jax.experimental import pallas as pl
from jax.experimental.pallas import tpu as pltpu
from jax.sharding import PartitionSpec as P

FIELDS = 5
LEVELS = 72
COARSEN = 4
ROWS = 16
COLS = 32
CYCLE = 512
HALF = 256
TOTAL_ROWS = 128
SHARE = 5
GROUP = 32
PLANES = FIELDS * SHARE
WIDE = 16
HALO = 4
BAND = ROWS + 2 * HALO
SLOTS = 4
KEPT = 448

diffusion = 0.2
advection_scale = 0.3
MIB = 2**20


def harmonics():
    column = np.arange(HALF)

    def wave(function, wavenumbers):
        angle = 2 * np.pi * ((column[:, None] * wavenumbers[None, :]) % CYCLE) / CYCLE
        scale = np.where((wavenumbers == 0) | (wavenumbers == HALF), 1.0, 2.0)
        return function(angle) * np.sqrt(scale / CYCLE)

    even_cos, even_sin = np.arange(0, HALF + 1, 2), np.arange(2, HALF, 2)
    odd = np.arange(1, HALF, 2)
    even = np.concatenate([wave(np.cos, even_cos), wave(np.sin, even_sin)], axis=1)
    odds = np.concatenate([wave(np.cos, odd), wave(np.sin, odd)], axis=1)
    order = np.concatenate([even_cos, even_sin, odd, odd])
    return even, odds, order


def stacked(matrix):
    high = matrix.astype(ml_dtypes.bfloat16)
    low = (matrix - high.astype(np.float64)).astype(ml_dtypes.bfloat16)
    return np.concatenate([high, low], axis=0)


EVEN, ODD, WAVES = harmonics()
BASIS = np.stack([stacked(EVEN), stacked(ODD), stacked(EVEN.T), stacked(ODD.T)])


def spreading():
    fine = np.arange(4 * COLS)
    matrix = np.zeros((4 * COLS, 4, 4 * COLS), np.float32)
    for part in range(4):
        matrix[part * COLS + fine // 4, part, fine] = 1.0
    matrix = matrix.reshape(4 * COLS, 16 * COLS)
    return np.concatenate([matrix, matrix]).astype(ml_dtypes.bfloat16)


def params(mib):
    return pltpu.CompilerParams(vmem_limit_bytes=mib * MIB)


def estimate(micros):
    return pl.CostEstimate(flops=int(micros * 1e9), bytes_accessed=int(micros * 1e6), transcendentals=0)


def scatter_levels(turned_ref, send_ref, fields, groups):
    size = groups * GROUP
    half_count = WIDE // 2

    def scatter(flip):
        for field in range(fields):
            for group in range(groups):
                for owner in range(pl.cdiv(LEVELS, SHARE)):
                    value = turned_ref[field * groups + group, SHARE * owner : SHARE * owner + SHARE, :]
                    at = (owner ^ (half_count * flip)) * size + group * GROUP + field * SHARE
                    send_ref[at : at + SHARE, :] = value

    flipped = lax.axis_index("narrow") >= lax.axis_size("narrow") // 2

    @pl.when(flipped)
    def _():
        scatter(1)

    @pl.when(jnp.logical_not(flipped))
    def _():
        scatter(0)


def pooling():
    fine = lax.broadcasted_iota(jnp.int32, (16 * COLS, 4 * COLS), 0)
    lane = lax.broadcasted_iota(jnp.int32, (16 * COLS, 4 * COLS), 1)
    meets = (fine // (4 * COLS) == lane // COLS) & ((fine % (4 * COLS)) // 4 == lane % COLS)
    return jnp.where(meets, 1.0 / 16, 0.0)


def pack_state(back_in, traj_in, send_ref, turned_ref, fine_ref, back_ref, wind_ref, sems):
    copies = [pltpu.make_async_copy(traj_in.at[0], wind_ref, sems.at[FIELDS])]
    copies += [pltpu.make_async_copy(back_in.at[f], back_ref.at[f], sems.at[f]) for f in range(FIELDS)]
    for copy in copies:
        copy.start()
    spare = jnp.zeros((8, 128), jnp.float32)
    pool = pooling()
    copies[0].wait()
    fine_ref[...] = wind_ref[...].astype(jnp.float32).reshape(LEVELS * 64, 128)
    for group in range(4):
        for field in range(FIELDS):
            if group == 0:
                copies[1 + field].wait()
            block = back_ref[field, 4 * group : 4 * group + 4].reshape(4 * COLS, LEVELS)
            turned_ref[field * 4 + group, 0:LEVELS, :] = block.T
            turned_ref[field * 4 + group, LEVELS:, :] = spare
        parts = []
        for part in range(4):
            first = 16 * group + 4 * part
            total = fine_ref[pl.ds(first, LEVELS, stride=64), :]
            for extra in range(1, 4):
                total = total + fine_ref[pl.ds(first + extra, LEVELS, stride=64), :]
            parts.append(total)
        mean = jnp.dot(
            jnp.concatenate(parts, axis=1),
            pool,
            precision=lax.Precision.HIGHEST,
            preferred_element_type=jnp.float32,
        )
        turned_ref[FIELDS * 4 + group, 0:LEVELS, :] = advection_scale * jnp.tanh(mean)
        turned_ref[FIELDS * 4 + group, LEVELS:, :] = spare
    scatter_levels(turned_ref, send_ref, FIELDS + 1, 4)


def pack_departures(place_ref, innov_ref, weight_ref, near_ref, far_ref, send_ref, turned_ref):
    spare = jnp.zeros((8, 128), jnp.float32)
    for field in range(FIELDS + 1):
        source = innov_ref.at[field] if field < FIELDS else weight_ref
        for group in range(5):
            if group < 4:
                block = source[4 * group : 4 * group + 4].reshape(4 * COLS, LEVELS)
            else:
                near, far = near_ref[field], far_ref[field]
                before = jnp.where(place_ref[3] == 1, near, far)
                after = jnp.where(place_ref[3] == 1, far, near)
                block = jnp.concatenate([before, after], axis=0).reshape(4 * COLS, LEVELS)
            turned_ref[field * 5 + group, 0:LEVELS, :] = block.T
            turned_ref[field * 5 + group, LEVELS:, :] = spare
    scatter_levels(turned_ref, send_ref, FIELDS + 1, 5)


def lane_block():
    return lax.broadcasted_iota(jnp.int32, (GROUP, 128), 1) // COLS


def turn(value, blocks):
    shift = (COLS * blocks) % 128
    return value if shift == 0 else pltpu.roll(value, shift, 1)


def unpack_rows(load, store):
    block = lane_block()
    for quarter in range(4):
        pieces = [load(4 * quarter + source) for source in range(4)]
        for row in range(4):
            value = turn(pieces[0], -row)
            for source in range(1, 4):
                value = jnp.where(block == source, turn(pieces[source], source - row), value)
            store(row, quarter, value)


def split_store(ref, at, value):
    high = value.astype(jnp.bfloat16)
    low = (value - high.astype(jnp.float32)).astype(jnp.bfloat16)
    ref[at, 0:HALF] = high
    ref[at, HALF:CYCLE] = low


def fold_store(even_ref, odd_ref, index, value):
    at = pl.ds(pl.multiple_of(index * GROUP, GROUP), GROUP)
    split_store(even_ref, at, value[:, :HALF] + value[:, HALF:])
    split_store(odd_ref, at, value[:, :HALF] - value[:, HALF:])


def product(ref, count, basis_ref, which):
    high, low = ref[0:count, 0:HALF], ref[0:count, HALF:CYCLE]
    basis_high, basis_low = basis_ref[which, 0:HALF], basis_ref[which, HALF:CYCLE]
    total = jnp.dot(high, basis_high, preferred_element_type=jnp.float32)
    total = total + jnp.dot(low, basis_high, preferred_element_type=jnp.float32)
    return total + jnp.dot(high, basis_low, preferred_element_type=jnp.float32)


def filtered(even_ref, odd_ref, basis_ref, resp_ref, first, rows, out_ref):
    count = rows * GROUP
    band = slice(first, first + rows)
    for ref, which, lanes in ((even_ref, 0, slice(0, HALF)), (odd_ref, 1, slice(HALF, CYCLE))):
        coefs = product(ref, count, basis_ref, which).reshape(rows, GROUP, HALF)
        coefs = (coefs * resp_ref[band, :, lanes]).reshape(count, HALF)
        split_store(ref, slice(0, count), coefs)
    even = product(even_ref, count, basis_ref, 2)
    odd = product(odd_ref, count, basis_ref, 3)
    out_ref[band, :, 0:HALF] = (even + odd).reshape(rows, GROUP, HALF)
    out_ref[band, :, HALF:CYCLE] = (even - odd).reshape(rows, GROUP, HALF)


def expand(source_ref, rows, out_ref):
    for field in range(FIELDS):
        out_ref[0:rows, SHARE * field : SHARE * field + SHARE, :] = source_ref[0:rows, PLANES : PLANES + SHARE, :]


def tangent(place_ref, recv_ref, near_ref, far_ref, resp_ref, basis_ref, kept_out, row_ref, state_ref, drift_ref, even_ref, odd_ref, sems):
    for group in range(6):
        def load(source):
            if group == 0:
                return jnp.where(place_ref[3] == 1, near_ref[source], far_ref[source])
            if group == 5:
                return jnp.where(place_ref[3] == 1, far_ref[source], near_ref[source])
            return recv_ref[source, GROUP * (group - 1) : GROUP * group, :]

        def store(row, quarter, value):
            row_ref[4 * group + row, :, 128 * quarter : 128 * quarter + 128] = value

        unpack_rows(load, store)
    drift_ref[:, GROUP - 8 :, :] = jnp.zeros((BAND, 8, CYCLE), jnp.float32)
    expand(row_ref, BAND, drift_ref)
    drift_copy = pltpu.make_async_copy(drift_ref, kept_out.at[BAND : 2 * BAND], sems.at[0])
    drift_copy.start()

    for step in range(2):
        first, last = 1 + step, BAND - 1 - step
        source_ref = row_ref if step == 0 else state_ref

        def body(index, carry):
            here = source_ref[index]
            east = pltpu.roll(here, CYCLE - 1, 1)
            west = pltpu.roll(here, 1, 1)
            near = source_ref[index - 1] + source_ref[index + 1] + east + west
            moved = here + diffusion * (near - 4.0 * here) + drift_ref[index] * (east - west)
            fold_store(even_ref, odd_ref, index - first, moved)
            return carry

        lax.fori_loop(first, last, body, 0, unroll=4)
        filtered(even_ref, odd_ref, basis_ref, resp_ref, first, last - first, state_ref)
    state_copy = pltpu.make_async_copy(state_ref, kept_out.at[0:BAND], sems.at[1])
    state_copy.start()
    drift_copy.wait()
    state_copy.wait()


def adjoint(place_ref, recv_ref, kept_in, traj_in, resp_ref, basis_ref, send_ref, held_ref, row_ref, field_ref, weight_ref, state_ref, drift_ref, even_ref, odd_ref, sems):
    held_copy = pltpu.make_async_copy(traj_in, held_ref, sems.at[2])
    state_copy = pltpu.make_async_copy(kept_in.at[0:BAND], state_ref, sems.at[0])
    state_copy.start()
    drift_copy = pltpu.make_async_copy(kept_in.at[BAND : 2 * BAND], drift_ref, sems.at[1])
    drift_copy.start()
    held_copy.start()
    for group in range(5):
        def load(source):
            return recv_ref[source, GROUP * group : GROUP * group + GROUP, :]

        def store(row, quarter, value):
            if group < 4:
                row_ref[4 * group + row + HALO, :, 128 * quarter : 128 * quarter + 128] = value
            else:
                at = 2 + row if row < 2 else 18 + row
                swapped = place_ref[1] if row < 2 else place_ref[2]
                lanes = pl.multiple_of(128 * ((quarter + 2 * swapped) & 3), 128)
                row_ref[at, :, pl.ds(lanes, 128)] = value

        unpack_rows(load, store)
    weight_ref[:, GROUP - 8 :, :] = jnp.zeros((BAND, 8, CYCLE), jnp.float32)
    for field in range(FIELDS):
        weight_ref[2:22, SHARE * field : SHARE * field + SHARE, :] = row_ref[2:22, PLANES : PLANES + SHARE, :]

    state_copy.wait()
    drift_copy.wait()

    def depart(index, carry):
        fold_store(even_ref, odd_ref, index - 2, weight_ref[index] * (state_ref[index] - row_ref[index]))
        return carry

    lax.fori_loop(2, 22, depart, 0, unroll=4)
    for step in range(2):
        first, last = 2 + step, BAND - 2 - step
        filtered(even_ref, odd_ref, basis_ref, resp_ref, first, last - first, field_ref)

        def body(index, carry):
            here = field_ref[index]
            carried = drift_ref[index] * here
            spread = diffusion * here
            moved = here + diffusion * (field_ref[index - 1] + field_ref[index + 1] - 4.0 * here)
            moved = moved + pltpu.roll(spread + carried, 1, 1) + pltpu.roll(spread - carried, CYCLE - 1, 1)
            if step == 0:
                fold_store(even_ref, odd_ref, index - 3, moved)
            else:
                row_ref[index] = moved
            return carry

        lax.fori_loop(first + 1, last - 1, body, 0, unroll=4)
    block = lane_block()
    for group in range(4):
        for quarter in range(4):
            lanes = slice(128 * quarter, 128 * quarter + 128)
            pieces = [row_ref[HALO + 4 * group + row, :, lanes] for row in range(4)]
            for source in range(4):
                value = turn(pieces[0], -source)
                for row in range(1, 4):
                    value = jnp.where(block == row, turn(pieces[row], row - source), value)
                send_ref[4 * quarter + source, PLANES * group : PLANES * group + PLANES, :] = value[:PLANES]
    held_copy.wait()


def prolong(place_ref, back_ref, cost_ref, traj_ref, spread_ref, out_ref, wide_ref, slot_ref, sems):
    whole, rest = LEVELS // SHARE, LEVELS % SHARE

    upper = lax.broadcasted_iota(jnp.int32, (8, 128), 0) < 4

    def fill(owner, slot, levels):
        source = (owner + (WIDE // 2) * place_ref[0]) & (WIDE - 1)
        for group in range(4):
            change = (
                back_ref[source, GROUP * group : GROUP * group + PLANES, :]
                - cost_ref[source, PLANES * group : PLANES * group + PLANES, :]
            )
            high = change.astype(jnp.bfloat16)
            low = (change - high.astype(jnp.float32)).astype(jnp.bfloat16)
            spread = jnp.dot(
                jnp.concatenate([high, low], axis=1), spread_ref[...], preferred_element_type=jnp.float32
            )
            for part in range(4):
                wide_ref[4 * group + part, 0:PLANES, :] = spread[:, 128 * part : 128 * part + 128]
        for field in range(FIELDS):
            for level in range(levels):
                plane = field * SHARE + level
                rows = []
                for pair in range(8):
                    above = jnp.broadcast_to(wide_ref[2 * pair, plane : plane + 1, :], (8, 128))
                    below = jnp.broadcast_to(wide_ref[2 * pair + 1, plane : plane + 1, :], (8, 128))
                    rows.append(jnp.where(upper, above, below))
                fine = jnp.concatenate(rows, axis=0)
                first_guess = traj_ref[field, SHARE * owner + level].astype(jnp.float32)
                slot_ref[slot, field, level] = (first_guess + fine).astype(jnp.bfloat16)

    def copy(owner, slot, levels=SHARE):
        return pltpu.make_async_copy(
            slot_ref.at[slot, :, 0:levels], out_ref.at[:, pl.ds(SHARE * owner, levels)], sems.at[slot]
        )

    for owner in range(SLOTS):
        fill(owner, owner, SHARE)
        copy(owner, owner).start()

    def body(owner, carry):
        slot = owner & (SLOTS - 1)
        copy(owner - SLOTS, slot).wait()
        fill(owner, slot, SHARE)
        copy(owner, slot).start()
        return carry

    lax.fori_loop(SLOTS, whole, body, 0)
    slot = whole % SLOTS
    copy(whole - SLOTS, slot).wait()
    fill(whole, slot, rest)
    copy(whole, slot, rest).start()
    for owner in range(whole - SLOTS + 1, whole):
        copy(owner, owner % SLOTS).wait()
    copy(whole, slot, rest).wait()


def response_rows(narrow_index):
    row = narrow_index * ROWS - HALO + jnp.arange(BAND, dtype=jnp.int32)
    latitude = jnp.pi * ((row.astype(jnp.float32) + 0.5) / TOTAL_ROWS - 0.5)
    cutoff = 0.5 * CYCLE * jnp.cos(latitude)
    inside = (row >= 0) & (row < TOTAL_ROWS)
    cutoff = jnp.where(inside, cutoff, 1.0)
    scaled = jnp.asarray(WAVES, jnp.float32)[None, :] / cutoff[:, None]
    response = jnp.where(inside[:, None], 1.0 / (1.0 + scaled**4), 0.0)
    return response.reshape(BAND, 1, CYCLE)


def shards(trajectory, innovation, background, obs_weight):
    f32 = jnp.float32
    narrow_count = lax.axis_size("narrow")
    narrow_index = lax.axis_index("narrow")
    middle = narrow_count // 2
    near, far = [], []
    for row in range(narrow_count - 1):
        for lane in range(WIDE):
            other = (lane + WIDE // 2) % WIDE if row == middle - 1 else lane
            one, two = lane * narrow_count + row, other * narrow_count + row + 1
            swaps = near if row % 2 == 0 else far
            swaps += [(one, two), (two, one)]
    odd = narrow_index % 2 == 1
    place = jnp.stack([narrow_index >= middle, narrow_index == middle, narrow_index == middle - 1, odd]).astype(jnp.int32)
    innov = innovation.transpose(0, 2, 3, 1)
    back = background.transpose(0, 2, 3, 1)
    weight = obs_weight.transpose(1, 2, 0)
    basis = jnp.asarray(BASIS)
    response = response_rows(narrow_index)

    def edge(rows):
        return jnp.concatenate([innov[:, rows], weight[None, rows]], axis=0)

    first, last = edge(slice(0, 2)), edge(slice(14, 16))
    edge_near = lax.ppermute(jnp.where(odd, first, last), ("wide", "narrow"), near)
    edge_far = lax.ppermute(jnp.where(odd, last, first), ("wide", "narrow"), far)

    full = pl.BlockSpec(memory_space=pltpu.VMEM)
    away = pl.BlockSpec(memory_space=pltpu.HBM)
    small = pl.BlockSpec(memory_space=pltpu.SMEM)
    send_state = pl.pallas_call(
        pack_state,
        in_specs=[away, away],
        out_specs=full,
        out_shape=jax.ShapeDtypeStruct((WIDE * 4 * GROUP, 128), f32),
        scratch_shapes=[
            pltpu.VMEM((24, 80, 128), f32),
            pltpu.VMEM((LEVELS * 64, 128), f32),
            pltpu.VMEM((FIELDS, ROWS, COLS, LEVELS), f32),
            pltpu.VMEM((LEVELS, 64, 128), jnp.bfloat16),
            pltpu.SemaphoreType.DMA((FIELDS + 1,)),
        ],
        compiler_params=params(60),
        cost_estimate=estimate(3),
    )(back, trajectory)
    send_state = send_state.reshape(WIDE, 4 * GROUP, 128)
    held_state = lax.all_to_all(send_state, "wide", split_axis=0, concat_axis=0, tiled=True)

    send_depart = pl.pallas_call(
        pack_departures,
        in_specs=[small] + [full] * 4,
        out_specs=full,
        out_shape=jax.ShapeDtypeStruct((WIDE * 5 * GROUP, 128), f32),
        scratch_shapes=[pltpu.VMEM((30, 80, 128), f32)],
        compiler_params=params(16),
        cost_estimate=estimate(3),
    )(place, innov, weight, edge_near, edge_far)
    send_depart = send_depart.reshape(WIDE, 5 * GROUP, 128)

    first, last = held_state[:, :GROUP], held_state[:, 3 * GROUP :]
    rows_near = lax.ppermute(jnp.where(odd, first, last), ("wide", "narrow"), near)
    rows_far = lax.ppermute(jnp.where(odd, last, first), ("wide", "narrow"), far)
    held_depart = lax.all_to_all(send_depart, "wide", split_axis=0, concat_axis=0, tiled=True)

    rows_shape = (BAND, GROUP, CYCLE)
    folded = pltpu.VMEM(((BAND - 2) * GROUP, CYCLE), jnp.bfloat16)
    kept = pl.pallas_call(
        tangent,
        in_specs=[small] + [full] * 5,
        out_specs=away,
        out_shape=jax.ShapeDtypeStruct((KEPT, GROUP, CYCLE), f32),
        scratch_shapes=[pltpu.VMEM(rows_shape, f32)] * 3 + [folded, folded, pltpu.SemaphoreType.DMA((2,))],
        compiler_params=params(40),
        cost_estimate=estimate(5),
    )(place, held_state, rows_near, rows_far, response, basis)
    send_cost, held = pl.pallas_call(
        adjoint,
        in_specs=[small, full, away, away, full, full],
        out_specs=[full, full],
        out_shape=[
            jax.ShapeDtypeStruct((WIDE, 4 * PLANES, 128), f32),
            jax.ShapeDtypeStruct(trajectory.shape, jnp.bfloat16),
        ],
        scratch_shapes=[pltpu.VMEM(rows_shape, f32)] * 5 + [folded, folded, pltpu.SemaphoreType.DMA((3,))],
        compiler_params=params(40),
        cost_estimate=estimate(5),
    )(place, held_depart, kept, trajectory, response, basis)
    costate = lax.all_to_all(send_cost, "wide", split_axis=0, concat_axis=0, tiled=True)

    return pl.pallas_call(
        prolong,
        in_specs=[small] + [full] * 4,
        out_specs=away,
        out_shape=jax.ShapeDtypeStruct(trajectory.shape, jnp.bfloat16),
        scratch_shapes=[
            pltpu.VMEM((16, GROUP, 128), f32),
            pltpu.VMEM((SLOTS, FIELDS, SHARE, 64, 128), jnp.bfloat16),
            pltpu.SemaphoreType.DMA((SLOTS,)),
        ],
        compiler_params=params(24),
        cost_estimate=estimate(5),
    )(place, send_state, costate, held, jnp.asarray(spreading()))


def solution(mesh):
    in_specs = (
        P(None, None, "narrow", "wide"),
        P(None, None, "narrow", "wide"),
        P(None, None, "narrow", "wide"),
        P(None, "narrow", "wide"),
    )
    out_specs = P(None, None, "narrow", "wide")
    return jax.shard_map(shards, mesh=mesh, in_specs=in_specs, out_specs=out_specs, check_vma=False)
```

```python
import jax
import jax.numpy as jnp
import ml_dtypes
import numpy as np
from jax import lax
from jax.experimental import pallas as pl
from jax.experimental.pallas import tpu as pltpu
from jax.sharding import PartitionSpec as P

FIELDS = 5
LEVELS = 72
COARSEN = 4
ROWS = 16
COLS = 32
CYCLE = 512
HALF = 256
TOTAL_ROWS = 128
SHARE = 5
GROUP = 32
PLANES = FIELDS * SHARE
SENT = PLANES + SHARE
STATE_ROWS, DEPART_ROWS = 4 * SENT, 5 * SENT + 2
WIDE = 16
HALO = 4
BAND = ROWS + 2 * HALO
SLOTS = 4
PITCH = 72
KEPT = 448

diffusion = 0.2
advection_scale = 0.3
MIB = 2**20


def harmonics():
    column = np.arange(HALF)

    def wave(function, wavenumbers):
        angle = 2 * np.pi * ((column[:, None] * wavenumbers[None, :]) % CYCLE) / CYCLE
        scale = np.where((wavenumbers == 0) | (wavenumbers == HALF), 1.0, 2.0)
        return function(angle) * np.sqrt(scale / CYCLE)

    even_cos, even_sin = np.arange(0, HALF + 1, 2), np.arange(2, HALF, 2)
    odd = np.arange(1, HALF, 2)
    even = np.concatenate([wave(np.cos, even_cos), wave(np.sin, even_sin)], axis=1)
    odds = np.concatenate([wave(np.cos, odd), wave(np.sin, odd)], axis=1)
    order = np.concatenate([even_cos, even_sin, odd, odd])
    return even, odds, order


def stacked(matrix):
    high = matrix.astype(ml_dtypes.bfloat16)
    low = (matrix - high.astype(np.float64)).astype(ml_dtypes.bfloat16)
    return np.concatenate([high, low], axis=0)


EVEN, ODD, WAVES = harmonics()
BASIS = np.stack([stacked(EVEN), stacked(ODD), stacked(EVEN.T), stacked(ODD.T)])


def spreading():
    fine = np.arange(4 * COLS)
    matrix = np.zeros((4 * COLS, 4, 4 * COLS), np.float32)
    for part in range(4):
        matrix[part * COLS + fine // 4, part, fine] = 1.0
    matrix = matrix.reshape(4 * COLS, 16 * COLS)
    return np.concatenate([matrix, matrix]).astype(ml_dtypes.bfloat16)


def params(mib):
    return pltpu.CompilerParams(vmem_limit_bytes=mib * MIB)


def estimate(micros):
    return pl.CostEstimate(flops=int(micros * 1e9), bytes_accessed=int(micros * 1e6), transcendentals=0)


def scatter_levels(turned_ref, send_ref, fields, groups, size):
    half_count = WIDE // 2

    def scatter(flip):
        for field in range(fields):
            for group in range(groups):
                for owner in range(pl.cdiv(LEVELS, SHARE)):
                    value = turned_ref[field * groups + group, SHARE * owner : SHARE * owner + SHARE, :]
                    at = (owner ^ (half_count * flip)) * size + group * SENT + field * SHARE
                    send_ref[at : at + SHARE, :] = value

    flipped = lax.axis_index("narrow") >= lax.axis_size("narrow") // 2

    @pl.when(flipped)
    def _():
        scatter(1)

    @pl.when(jnp.logical_not(flipped))
    def _():
        scatter(0)


def pooling():
    fine = lax.broadcasted_iota(jnp.int32, (16 * COLS, 4 * COLS), 0)
    lane = lax.broadcasted_iota(jnp.int32, (16 * COLS, 4 * COLS), 1)
    meets = (fine // (4 * COLS) == lane // COLS) & ((fine % (4 * COLS)) // 4 == lane % COLS)
    return jnp.where(meets, 1.0 / 16, 0.0).astype(jnp.bfloat16)


def pack_state(back_in, traj_in, send_ref, turned_ref, fine_ref, back_ref, wind_ref, sems):
    copies = [pltpu.make_async_copy(traj_in.at[0], wind_ref, sems.at[FIELDS])]
    copies += [pltpu.make_async_copy(back_in.at[f], back_ref.at[f], sems.at[f]) for f in range(FIELDS)]
    for copy in copies:
        copy.start()
    spare = jnp.zeros((8, 128), jnp.float32)
    pool = pooling()
    copies[0].wait()
    for level in range(LEVELS):
        fine_ref[PITCH * level : PITCH * level + 64, :] = wind_ref[level].astype(jnp.float32)
    for group in range(4):
        for field in range(FIELDS):
            if group == 0:
                copies[1 + field].wait()
            block = back_ref[field, 4 * group : 4 * group + 4].reshape(4 * COLS, LEVELS)
            turned_ref[field * 4 + group, 0:LEVELS, :] = block.T
            turned_ref[field * 4 + group, LEVELS:, :] = spare
        parts = []
        for part in range(4):
            first = 16 * group + 4 * part
            total = fine_ref[pl.ds(first, LEVELS, stride=PITCH), :]
            for extra in range(1, 4):
                total = total + fine_ref[pl.ds(first + extra, LEVELS, stride=PITCH), :]
            parts.append(total)
        total = jnp.concatenate(parts, axis=1)
        high = total.astype(jnp.bfloat16)
        low = (total - high.astype(jnp.float32)).astype(jnp.bfloat16)
        mean = jnp.dot(high, pool, preferred_element_type=jnp.float32)
        mean = mean + jnp.dot(low, pool, preferred_element_type=jnp.float32)
        turned_ref[FIELDS * 4 + group, 0:LEVELS, :] = advection_scale * jnp.tanh(mean)
        turned_ref[FIELDS * 4 + group, LEVELS:, :] = spare
    scatter_levels(turned_ref, send_ref, FIELDS + 1, 4, STATE_ROWS)


def pack_departures(place_ref, innov_ref, weight_ref, near_ref, far_ref, send_ref, turned_ref):
    spare = jnp.zeros((8, 128), jnp.float32)
    for field in range(FIELDS + 1):
        source = innov_ref.at[field] if field < FIELDS else weight_ref
        for group in range(5):
            if group < 4:
                block = source[4 * group : 4 * group + 4].reshape(4 * COLS, LEVELS)
            else:
                near, far = near_ref[field], far_ref[field]
                before = jnp.where(place_ref[3] == 1, near, far)
                after = jnp.where(place_ref[3] == 1, far, near)
                block = jnp.concatenate([before, after], axis=0).reshape(4 * COLS, LEVELS)
            turned_ref[field * 5 + group, 0:LEVELS, :] = block.T
            turned_ref[field * 5 + group, LEVELS:, :] = spare
    scatter_levels(turned_ref, send_ref, FIELDS + 1, 5, DEPART_ROWS)


def lane_block():
    return lax.broadcasted_iota(jnp.int32, (GROUP, 128), 1) // COLS


def turn(value, blocks):
    shift = (COLS * blocks) % 128
    return value if shift == 0 else pltpu.roll(value, shift, 1)


def unpack_rows(load, store):
    block = lane_block()
    for quarter in range(4):
        pieces = [load(4 * quarter + source) for source in range(4)]
        for row in range(4):
            value = turn(pieces[0], -row)
            for source in range(1, 4):
                value = jnp.where(block == source, turn(pieces[source], source - row), value)
            store(row, quarter, value)


def split_store(ref, at, value):
    high = value.astype(jnp.bfloat16)
    low = (value - high.astype(jnp.float32)).astype(jnp.bfloat16)
    ref[at, 0:HALF] = high
    ref[at, HALF:CYCLE] = low


def fold_store(even_ref, odd_ref, index, value):
    at = pl.ds(pl.multiple_of(index * GROUP, GROUP), GROUP)
    split_store(even_ref, at, value[:, :HALF] + value[:, HALF:])
    split_store(odd_ref, at, value[:, :HALF] - value[:, HALF:])


def product(ref, count, basis_ref, which):
    high, low = ref[0:count, 0:HALF], ref[0:count, HALF:CYCLE]
    basis_high, basis_low = basis_ref[which, 0:HALF], basis_ref[which, HALF:CYCLE]
    total = jnp.dot(high, basis_high, preferred_element_type=jnp.float32)
    total = total + jnp.dot(low, basis_high, preferred_element_type=jnp.float32)
    return total + jnp.dot(high, basis_low, preferred_element_type=jnp.float32)


def filtered(even_ref, odd_ref, basis_ref, resp_ref, first, rows, out_ref):
    count = rows * GROUP
    band = slice(first, first + rows)
    for ref, which, lanes in ((even_ref, 0, slice(0, HALF)), (odd_ref, 1, slice(HALF, CYCLE))):
        coefs = product(ref, count, basis_ref, which).reshape(rows, GROUP, HALF)
        coefs = (coefs * resp_ref[band, :, lanes]).reshape(count, HALF)
        split_store(ref, slice(0, count), coefs)
    even = product(even_ref, count, basis_ref, 2)
    odd = product(odd_ref, count, basis_ref, 3)
    out_ref[band, :, 0:HALF] = (even + odd).reshape(rows, GROUP, HALF)
    out_ref[band, :, HALF:CYCLE] = (even - odd).reshape(rows, GROUP, HALF)


def expand(source_ref, rows, out_ref):
    for field in range(FIELDS):
        out_ref[0:rows, SHARE * field : SHARE * field + SHARE, :] = source_ref[0:rows, PLANES : PLANES + SHARE, :]


def tangent(place_ref, recv_ref, near_ref, far_ref, resp_ref, basis_ref, kept_out, row_ref, state_ref, drift_ref, even_ref, odd_ref, sems):
    for group in range(6):
        def load(source):
            if group == 0:
                return jnp.where(place_ref[3] == 1, near_ref[source], far_ref[source])
            if group == 5:
                return jnp.where(place_ref[3] == 1, far_ref[source], near_ref[source])
            first = SENT * (group - 1) if group < 4 else STATE_ROWS - GROUP
            return recv_ref[source, first : first + GROUP, :]

        def store(row, quarter, value):
            lanes = slice(128 * quarter, 128 * quarter + 128)
            if group in (0, 4):
                row_ref[4 * group + row, 0:SENT, lanes] = value[GROUP - SENT :]
            else:
                row_ref[4 * group + row, :, lanes] = value

        unpack_rows(load, store)
    drift_ref[:, GROUP - 8 :, :] = jnp.zeros((BAND, 8, CYCLE), jnp.float32)
    expand(row_ref, BAND, drift_ref)
    drift_copy = pltpu.make_async_copy(drift_ref, kept_out.at[BAND : 2 * BAND], sems.at[0])
    drift_copy.start()

    for step in range(2):
        first, last = 1 + step, BAND - 1 - step
        source_ref = row_ref if step == 0 else state_ref

        def body(index, carry):
            here = source_ref[index]
            east = pltpu.roll(here, CYCLE - 1, 1)
            west = pltpu.roll(here, 1, 1)
            near = source_ref[index - 1] + source_ref[index + 1] + east + west
            moved = here + diffusion * (near - 4.0 * here) + drift_ref[index] * (east - west)
            fold_store(even_ref, odd_ref, index - first, moved)
            return carry

        lax.fori_loop(first, last, body, 0, unroll=4)
        filtered(even_ref, odd_ref, basis_ref, resp_ref, first, last - first, state_ref)
    state_copy = pltpu.make_async_copy(state_ref, kept_out.at[0:BAND], sems.at[1])
    state_copy.start()
    drift_copy.wait()
    state_copy.wait()


def adjoint(place_ref, recv_ref, kept_in, traj_in, resp_ref, basis_ref, send_ref, held_ref, row_ref, field_ref, weight_ref, state_ref, drift_ref, even_ref, odd_ref, sems):
    held_copy = pltpu.make_async_copy(traj_in, held_ref, sems.at[2])
    state_copy = pltpu.make_async_copy(kept_in.at[0:BAND], state_ref, sems.at[0])
    state_copy.start()
    drift_copy = pltpu.make_async_copy(kept_in.at[BAND : 2 * BAND], drift_ref, sems.at[1])
    drift_copy.start()
    held_copy.start()
    for group in range(5):
        def load(source):
            return recv_ref[source, SENT * group : SENT * group + GROUP, :]

        def store(row, quarter, value):
            if group < 4:
                row_ref[4 * group + row + HALO, :, 128 * quarter : 128 * quarter + 128] = value
            else:
                at = 2 + row if row < 2 else 18 + row
                swapped = place_ref[1] if row < 2 else place_ref[2]
                lanes = pl.multiple_of(128 * ((quarter + 2 * swapped) & 3), 128)
                row_ref[at, :, pl.ds(lanes, 128)] = value

        unpack_rows(load, store)
    weight_ref[:, GROUP - 8 :, :] = jnp.zeros((BAND, 8, CYCLE), jnp.float32)
    for field in range(FIELDS):
        weight_ref[2:22, SHARE * field : SHARE * field + SHARE, :] = row_ref[2:22, PLANES : PLANES + SHARE, :]

    state_copy.wait()
    drift_copy.wait()

    def depart(index, carry):
        fold_store(even_ref, odd_ref, index - 2, weight_ref[index] * (state_ref[index] - row_ref[index]))
        return carry

    lax.fori_loop(2, 22, depart, 0, unroll=4)
    for step in range(2):
        first, last = 2 + step, BAND - 2 - step
        filtered(even_ref, odd_ref, basis_ref, resp_ref, first, last - first, field_ref)

        def body(index, carry):
            here = field_ref[index]
            carried = drift_ref[index] * here
            spread = diffusion * here
            moved = here + diffusion * (field_ref[index - 1] + field_ref[index + 1] - 4.0 * here)
            moved = moved + pltpu.roll(spread + carried, 1, 1) + pltpu.roll(spread - carried, CYCLE - 1, 1)
            if step == 0:
                fold_store(even_ref, odd_ref, index - 3, moved)
            else:
                row_ref[index] = moved
            return carry

        lax.fori_loop(first + 1, last - 1, body, 0, unroll=4)
    block = lane_block()
    for group in range(4):
        for quarter in range(4):
            lanes = slice(128 * quarter, 128 * quarter + 128)
            pieces = [row_ref[HALO + 4 * group + row, :, lanes] for row in range(4)]
            for source in range(4):
                value = turn(pieces[0], -source)
                for row in range(1, 4):
                    value = jnp.where(block == row, turn(pieces[row], row - source), value)
                send_ref[4 * quarter + source, PLANES * group : PLANES * group + PLANES, :] = value[:PLANES]
    held_copy.wait()


def prolong(place_ref, back_ref, cost_ref, traj_ref, spread_ref, out_ref, wide_ref, slot_ref, sems):
    whole, rest = LEVELS // SHARE, LEVELS % SHARE

    upper = lax.broadcasted_iota(jnp.int32, (8, 128), 0) < 4

    def fill(owner, slot, levels):
        source = (owner + (WIDE // 2) * place_ref[0]) & (WIDE - 1)
        for group in range(4):
            change = (
                back_ref[source, SENT * group : SENT * group + PLANES, :]
                - cost_ref[source, PLANES * group : PLANES * group + PLANES, :]
            )
            high = change.astype(jnp.bfloat16)
            low = (change - high.astype(jnp.float32)).astype(jnp.bfloat16)
            spread = jnp.dot(
                jnp.concatenate([high, low], axis=1), spread_ref[...], preferred_element_type=jnp.float32
            )
            for part in range(4):
                wide_ref[4 * group + part, 0:PLANES, :] = spread[:, 128 * part : 128 * part + 128]
        for field in range(FIELDS):
            for level in range(levels):
                plane = field * SHARE + level
                rows = []
                for pair in range(8):
                    above = jnp.broadcast_to(wide_ref[2 * pair, plane : plane + 1, :], (8, 128))
                    below = jnp.broadcast_to(wide_ref[2 * pair + 1, plane : plane + 1, :], (8, 128))
                    rows.append(jnp.where(upper, above, below))
                fine = jnp.concatenate(rows, axis=0)
                first_guess = traj_ref[field, SHARE * owner + level].astype(jnp.float32)
                slot_ref[slot, field, level] = (first_guess + fine).astype(jnp.bfloat16)

    def copy(owner, slot, levels=SHARE):
        return pltpu.make_async_copy(
            slot_ref.at[slot, :, 0:levels], out_ref.at[:, pl.ds(SHARE * owner, levels)], sems.at[slot]
        )

    for owner in range(SLOTS):
        fill(owner, owner, SHARE)
        copy(owner, owner).start()

    def body(owner, carry):
        slot = owner & (SLOTS - 1)
        copy(owner - SLOTS, slot).wait()
        fill(owner, slot, SHARE)
        copy(owner, slot).start()
        return carry

    lax.fori_loop(SLOTS, whole, body, 0)
    slot = whole % SLOTS
    copy(whole - SLOTS, slot).wait()
    fill(whole, slot, rest)
    copy(whole, slot, rest).start()
    for owner in range(whole - SLOTS + 1, whole):
        copy(owner, owner % SLOTS).wait()
    copy(whole, slot, rest).wait()


def response_rows(narrow_index):
    row = narrow_index * ROWS - HALO + jnp.arange(BAND, dtype=jnp.int32)
    latitude = jnp.pi * ((row.astype(jnp.float32) + 0.5) / TOTAL_ROWS - 0.5)
    cutoff = 0.5 * CYCLE * jnp.cos(latitude)
    inside = (row >= 0) & (row < TOTAL_ROWS)
    cutoff = jnp.where(inside, cutoff, 1.0)
    scaled = jnp.asarray(WAVES, jnp.float32)[None, :] / cutoff[:, None]
    response = jnp.where(inside[:, None], 1.0 / (1.0 + scaled**4), 0.0)
    return response.reshape(BAND, 1, CYCLE)


def shards(trajectory, innovation, background, obs_weight):
    f32 = jnp.float32
    narrow_count = lax.axis_size("narrow")
    narrow_index = lax.axis_index("narrow")
    middle = narrow_count // 2
    near, far = [], []
    for row in range(narrow_count - 1):
        for lane in range(WIDE):
            other = (lane + WIDE // 2) % WIDE if row == middle - 1 else lane
            one, two = lane * narrow_count + row, other * narrow_count + row + 1
            swaps = near if row % 2 == 0 else far
            swaps += [(one, two), (two, one)]
    odd = narrow_index % 2 == 1
    place = jnp.stack([narrow_index >= middle, narrow_index == middle, narrow_index == middle - 1, odd]).astype(jnp.int32)
    innov = innovation.transpose(0, 2, 3, 1)
    back = background.transpose(0, 2, 3, 1)
    weight = obs_weight.transpose(1, 2, 0)
    basis = jnp.asarray(BASIS)
    response = response_rows(narrow_index)

    def edge(rows):
        return jnp.concatenate([innov[:, rows], weight[None, rows]], axis=0)

    first, last = edge(slice(0, 2)), edge(slice(14, 16))
    edge_near = lax.ppermute(jnp.where(odd, first, last), ("wide", "narrow"), near)
    edge_far = lax.ppermute(jnp.where(odd, last, first), ("wide", "narrow"), far)

    full = pl.BlockSpec(memory_space=pltpu.VMEM)
    away = pl.BlockSpec(memory_space=pltpu.HBM)
    small = pl.BlockSpec(memory_space=pltpu.SMEM)
    send_state = pl.pallas_call(
        pack_state,
        in_specs=[away, away],
        out_specs=full,
        out_shape=jax.ShapeDtypeStruct((WIDE * STATE_ROWS, 128), f32),
        scratch_shapes=[
            pltpu.VMEM((24, 80, 128), f32),
            pltpu.VMEM((LEVELS * PITCH, 128), f32),
            pltpu.VMEM((FIELDS, ROWS, COLS, LEVELS), f32),
            pltpu.VMEM((LEVELS, 64, 128), jnp.bfloat16),
            pltpu.SemaphoreType.DMA((FIELDS + 1,)),
        ],
        compiler_params=params(60),
        cost_estimate=estimate(3),
    )(back, trajectory)
    send_state = send_state.reshape(WIDE, STATE_ROWS, 128)
    held_state = lax.all_to_all(send_state, "wide", split_axis=0, concat_axis=0, tiled=True)

    send_depart = pl.pallas_call(
        pack_departures,
        in_specs=[small] + [full] * 4,
        out_specs=full,
        out_shape=jax.ShapeDtypeStruct((WIDE * DEPART_ROWS, 128), f32),
        scratch_shapes=[pltpu.VMEM((30, 80, 128), f32)],
        compiler_params=params(16),
        cost_estimate=estimate(3),
    )(place, innov, weight, edge_near, edge_far)
    send_depart = send_depart.reshape(WIDE, DEPART_ROWS, 128)

    first, last = held_state[:, :GROUP], held_state[:, STATE_ROWS - GROUP :]
    rows_near = lax.ppermute(jnp.where(odd, first, last), ("wide", "narrow"), near)
    rows_far = lax.ppermute(jnp.where(odd, last, first), ("wide", "narrow"), far)
    held_depart = lax.all_to_all(send_depart, "wide", split_axis=0, concat_axis=0, tiled=True)

    rows_shape = (BAND, GROUP, CYCLE)
    folded = pltpu.VMEM(((BAND - 2) * GROUP, CYCLE), jnp.bfloat16)
    kept = pl.pallas_call(
        tangent,
        in_specs=[small] + [full] * 5,
        out_specs=away,
        out_shape=jax.ShapeDtypeStruct((KEPT, GROUP, CYCLE), f32),
        scratch_shapes=[pltpu.VMEM(rows_shape, f32)] * 3 + [folded, folded, pltpu.SemaphoreType.DMA((2,))],
        compiler_params=params(40),
        cost_estimate=estimate(5),
    )(place, held_state, rows_near, rows_far, response, basis)
    send_cost, held = pl.pallas_call(
        adjoint,
        in_specs=[small, full, away, away, full, full],
        out_specs=[full, full],
        out_shape=[
            jax.ShapeDtypeStruct((WIDE, 4 * PLANES, 128), f32),
            jax.ShapeDtypeStruct(trajectory.shape, jnp.bfloat16),
        ],
        scratch_shapes=[pltpu.VMEM(rows_shape, f32)] * 5 + [folded, folded, pltpu.SemaphoreType.DMA((3,))],
        compiler_params=params(40),
        cost_estimate=estimate(5),
    )(place, held_depart, kept, trajectory, response, basis)
    costate = lax.all_to_all(send_cost, "wide", split_axis=0, concat_axis=0, tiled=True)

    return pl.pallas_call(
        prolong,
        in_specs=[small] + [full] * 4,
        out_specs=away,
        out_shape=jax.ShapeDtypeStruct(trajectory.shape, jnp.bfloat16),
        scratch_shapes=[
            pltpu.VMEM((16, GROUP, 128), f32),
            pltpu.VMEM((SLOTS, FIELDS, SHARE, 64, 128), jnp.bfloat16),
            pltpu.SemaphoreType.DMA((SLOTS,)),
        ],
        compiler_params=params(24),
        cost_estimate=estimate(5),
    )(place, send_state, costate, held, jnp.asarray(spreading()))


def solution(mesh):
    in_specs = (
        P(None, None, "narrow", "wide"),
        P(None, None, "narrow", "wide"),
        P(None, None, "narrow", "wide"),
        P(None, "narrow", "wide"),
    )
    out_specs = P(None, None, "narrow", "wide")
    return jax.shard_map(shards, mesh=mesh, in_specs=in_specs, out_specs=out_specs, check_vma=False)
```

```python
import jax
import jax.numpy as jnp
import ml_dtypes
import numpy as np
from jax import lax
from jax.experimental import pallas as pl
from jax.experimental.pallas import tpu as pltpu
from jax.sharding import PartitionSpec as P

FIELDS = 5
LEVELS = 72
COARSEN = 4
ROWS = 16
COLS = 32
CYCLE = 512
HALF = 256
TOTAL_ROWS = 128
SHARE = 5
GROUP = 32
PLANES = FIELDS * SHARE
SENT = PLANES + SHARE
STATE_ROWS, DEPART_ROWS = 4 * SENT, 5 * SENT + 2
WIDE = 16
HALO = 4
BAND = ROWS + 2 * HALO
SLOTS = 4
PITCH = 72
KEPT = 448

diffusion = 0.2
advection_scale = 0.3
MIB = 2**20


def harmonics():
    column = np.arange(HALF)

    def wave(function, wavenumbers):
        angle = 2 * np.pi * ((column[:, None] * wavenumbers[None, :]) % CYCLE) / CYCLE
        scale = np.where((wavenumbers == 0) | (wavenumbers == HALF), 1.0, 2.0)
        return function(angle) * np.sqrt(scale / CYCLE)

    even_cos, even_sin = np.arange(0, HALF + 1, 2), np.arange(2, HALF, 2)
    odd = np.arange(1, HALF, 2)
    even = np.concatenate([wave(np.cos, even_cos), wave(np.sin, even_sin)], axis=1)
    odds = np.concatenate([wave(np.cos, odd), wave(np.sin, odd)], axis=1)
    order = np.concatenate([even_cos, even_sin, odd, odd])
    return even, odds, order


def stacked(matrix):
    high = matrix.astype(ml_dtypes.bfloat16)
    low = (matrix - high.astype(np.float64)).astype(ml_dtypes.bfloat16)
    return np.concatenate([high, low], axis=0)


EVEN, ODD, WAVES = harmonics()
BASIS = np.stack([stacked(EVEN), stacked(ODD), stacked(EVEN.T), stacked(ODD.T)])


def spreading():
    fine = np.arange(4 * COLS)
    matrix = np.zeros((4 * COLS, 4, 4 * COLS), np.float32)
    for part in range(4):
        matrix[part * COLS + fine // 4, part, fine] = 1.0
    matrix = matrix.reshape(4 * COLS, 16 * COLS)
    return np.concatenate([matrix, matrix]).astype(ml_dtypes.bfloat16)


def params(mib):
    return pltpu.CompilerParams(vmem_limit_bytes=mib * MIB)


def estimate(micros):
    return pl.CostEstimate(flops=int(micros * 1e9), bytes_accessed=int(micros * 1e6), transcendentals=0)


def scatter_levels(turned_ref, send_ref, fields, groups, size):
    half_count = WIDE // 2

    def scatter(flip):
        for field in range(fields):
            for group in range(groups):
                for owner in range(pl.cdiv(LEVELS, SHARE)):
                    value = turned_ref[field * groups + group, SHARE * owner : SHARE * owner + SHARE, :]
                    at = (owner ^ (half_count * flip)) * size + group * SENT + field * SHARE
                    send_ref[at : at + SHARE, :] = value

    flipped = lax.axis_index("narrow") >= lax.axis_size("narrow") // 2

    @pl.when(flipped)
    def _():
        scatter(1)

    @pl.when(jnp.logical_not(flipped))
    def _():
        scatter(0)


def pooling():
    fine = lax.broadcasted_iota(jnp.int32, (16 * COLS, 4 * COLS), 0)
    lane = lax.broadcasted_iota(jnp.int32, (16 * COLS, 4 * COLS), 1)
    meets = (fine // (4 * COLS) == lane // COLS) & ((fine % (4 * COLS)) // 4 == lane % COLS)
    return jnp.where(meets, 1.0 / 16, 0.0).astype(jnp.bfloat16)


def pack_state(
    back_in, traj_in, innov_in, weight_in, send_ref, near_out, far_out, turned_ref, fine_ref, back_ref, wind_ref, edge_ref, sems
):
    copies = [pltpu.make_async_copy(traj_in.at[0], wind_ref, sems.at[FIELDS])]
    copies += [pltpu.make_async_copy(back_in.at[f], back_ref.at[f], sems.at[f]) for f in range(FIELDS)]
    for copy in copies:
        copy.start()
    odd = lax.axis_index("narrow") % 2
    edges, leaving = [], []
    for side, (out_ref, row) in enumerate(((near_out, 14 - 14 * odd), (far_out, 14 * odd))):
        at = FIELDS + 1 + 3 * side
        held = edge_ref.at[side]
        edges.append(pltpu.make_async_copy(innov_in.at[:, pl.ds(row, 2)], held.at[0:FIELDS], sems.at[at]))
        edges.append(pltpu.make_async_copy(weight_in.at[pl.ds(row, 2)], held.at[FIELDS], sems.at[at + 1]))
        leaving.append(pltpu.make_async_copy(held, out_ref, sems.at[at + 2]))
    for copy in edges:
        copy.start()
    spare = jnp.zeros((8, 128), jnp.float32)
    pool = pooling()
    copies[0].wait()
    for level in range(LEVELS):
        fine_ref[PITCH * level : PITCH * level + 64, :] = wind_ref[level].astype(jnp.float32)
    for group in range(4):
        for field in range(FIELDS):
            if group == 0:
                copies[1 + field].wait()
            block = back_ref[field, 4 * group : 4 * group + 4].reshape(4 * COLS, LEVELS)
            turned_ref[field * 4 + group, 0:LEVELS, :] = block.T
            turned_ref[field * 4 + group, LEVELS:, :] = spare
        parts = []
        for part in range(4):
            first = 16 * group + 4 * part
            total = fine_ref[pl.ds(first, LEVELS, stride=PITCH), :]
            for extra in range(1, 4):
                total = total + fine_ref[pl.ds(first + extra, LEVELS, stride=PITCH), :]
            parts.append(total)
        total = jnp.concatenate(parts, axis=1)
        high = total.astype(jnp.bfloat16)
        low = (total - high.astype(jnp.float32)).astype(jnp.bfloat16)
        mean = jnp.dot(high, pool, preferred_element_type=jnp.float32)
        mean = mean + jnp.dot(low, pool, preferred_element_type=jnp.float32)
        turned_ref[FIELDS * 4 + group, 0:LEVELS, :] = advection_scale * jnp.tanh(mean)
        turned_ref[FIELDS * 4 + group, LEVELS:, :] = spare
    for copy in edges:
        copy.wait()
    for copy in leaving:
        copy.start()
    scatter_levels(turned_ref, send_ref, FIELDS + 1, 4, STATE_ROWS)
    for copy in leaving:
        copy.wait()


def pack_departures(place_ref, innov_ref, weight_ref, near_ref, far_ref, send_ref, turned_ref):
    spare = jnp.zeros((8, 128), jnp.float32)
    for field in range(FIELDS + 1):
        source = innov_ref.at[field] if field < FIELDS else weight_ref
        for group in range(5):
            if group < 4:
                block = source[4 * group : 4 * group + 4].reshape(4 * COLS, LEVELS)
            else:
                near, far = near_ref[field], far_ref[field]
                before = jnp.where(place_ref[3] == 1, near, far)
                after = jnp.where(place_ref[3] == 1, far, near)
                block = jnp.concatenate([before, after], axis=0).reshape(4 * COLS, LEVELS)
            turned_ref[field * 5 + group, 0:LEVELS, :] = block.T
            turned_ref[field * 5 + group, LEVELS:, :] = spare
    scatter_levels(turned_ref, send_ref, FIELDS + 1, 5, DEPART_ROWS)


def lane_block():
    return lax.broadcasted_iota(jnp.int32, (GROUP, 128), 1) // COLS


def turn(value, blocks):
    shift = (COLS * blocks) % 128
    return value if shift == 0 else pltpu.roll(value, shift, 1)


def unpack_rows(load, store):
    block = lane_block()
    for quarter in range(4):
        pieces = [load(4 * quarter + source) for source in range(4)]
        for row in range(4):
            value = turn(pieces[0], -row)
            for source in range(1, 4):
                value = jnp.where(block == source, turn(pieces[source], source - row), value)
            store(row, quarter, value)


def split_store(ref, at, value):
    high = value.astype(jnp.bfloat16)
    low = (value - high.astype(jnp.float32)).astype(jnp.bfloat16)
    ref[at, 0:HALF] = high
    ref[at, HALF:CYCLE] = low


def fold_store(even_ref, odd_ref, index, value):
    at = pl.ds(pl.multiple_of(index * GROUP, GROUP), GROUP)
    split_store(even_ref, at, value[:, :HALF] + value[:, HALF:])
    split_store(odd_ref, at, value[:, :HALF] - value[:, HALF:])


def product(ref, count, basis_ref, which):
    high, low = ref[0:count, 0:HALF], ref[0:count, HALF:CYCLE]
    basis_high, basis_low = basis_ref[which, 0:HALF], basis_ref[which, HALF:CYCLE]
    total = jnp.dot(high, basis_high, preferred_element_type=jnp.float32)
    total = total + jnp.dot(low, basis_high, preferred_element_type=jnp.float32)
    return total + jnp.dot(high, basis_low, preferred_element_type=jnp.float32)


def filtered(even_ref, odd_ref, basis_ref, resp_ref, bands, out_ref):
    rows = sum(last - first for first, last in bands)
    count = rows * GROUP
    for ref, which, lanes in ((even_ref, 0, slice(0, HALF)), (odd_ref, 1, slice(HALF, CYCLE))):
        scale = [resp_ref[first:last, :, lanes] for first, last in bands]
        scale = scale[0] if len(scale) == 1 else jnp.concatenate(scale, axis=0)
        coefs = product(ref, count, basis_ref, which).reshape(rows, GROUP, HALF)
        split_store(ref, slice(0, count), (coefs * scale).reshape(count, HALF))
    even = product(even_ref, count, basis_ref, 2)
    odd = product(odd_ref, count, basis_ref, 3)
    plus, minus = (even + odd).reshape(rows, GROUP, HALF), (even - odd).reshape(rows, GROUP, HALF)
    start = 0
    for first, last in bands:
        size = last - first
        out_ref[first:last, :, 0:HALF] = plus[start : start + size]
        out_ref[first:last, :, HALF:CYCLE] = minus[start : start + size]
        start += size


def expand(source_ref, first, last, out_ref):
    out_ref[first:last, GROUP - 8 :, :] = jnp.zeros((last - first, 8, CYCLE), jnp.float32)
    for field in range(FIELDS):
        part = slice(SHARE * field, SHARE * field + SHARE)
        out_ref[first:last, part, :] = source_ref[first:last, PLANES : PLANES + SHARE, :]


def moved_rows(source_ref, drift_ref, even_ref, odd_ref, first, last, offset):
    def body(index, carry):
        here = source_ref[index]
        east = pltpu.roll(here, CYCLE - 1, 1)
        west = pltpu.roll(here, 1, 1)
        near = source_ref[index - 1] + source_ref[index + 1] + east + west
        moved = here + diffusion * (near - 4.0 * here) + drift_ref[index] * (east - west)
        fold_store(even_ref, odd_ref, index - first + offset, moved)
        return carry

    lax.fori_loop(first, last, body, 0, unroll=4)


def unpack_state(load, row_ref, group):
    def store(row, quarter, value):
        lanes = slice(128 * quarter, 128 * quarter + 128)
        if group in (0, 4):
            row_ref[4 * group + row, 0:SENT, lanes] = value[GROUP - SENT :]
        else:
            row_ref[4 * group + row, :, lanes] = value

    unpack_rows(load, store)


STATE, DRIFT, RAW, STEPPED = 0, BAND, 2 * BAND, 3 * BAND


def tangent(recv_ref, resp_ref, basis_ref, kept_out, row_ref, mid_ref, state_ref, drift_ref, even_ref, odd_ref, sems):
    copies = []

    def keep(ref, first, last, place):
        copy = pltpu.make_async_copy(
            ref.at[first:last], kept_out.at[place + first : place + last], sems.at[len(copies)]
        )
        copy.start()
        copies.append(copy)

    for group in range(1, 5):
        first = SENT * (group - 1) if group < 4 else STATE_ROWS - GROUP
        unpack_state(lambda source: recv_ref[source, first : first + GROUP, :], row_ref, group)
    expand(row_ref, 4, 20, drift_ref)
    keep(row_ref, 4, 6, RAW)
    keep(row_ref, 18, 20, RAW)
    keep(drift_ref, 4, 20, DRIFT)
    moved_rows(row_ref, drift_ref, even_ref, odd_ref, 5, 19, 0)
    filtered(even_ref, odd_ref, basis_ref, resp_ref, [(5, 19)], mid_ref)
    keep(mid_ref, 5, 7, STEPPED)
    keep(mid_ref, 17, 19, STEPPED)
    moved_rows(mid_ref, drift_ref, even_ref, odd_ref, 6, 18, 0)
    filtered(even_ref, odd_ref, basis_ref, resp_ref, [(6, 18)], state_ref)
    keep(state_ref, 6, 18, STATE)
    for copy in copies:
        copy.wait()


def tangent_edges(
    place_ref, near_ref, far_ref, resp_ref, basis_ref, kept_in, kept_out,
    row_ref, mid_ref, state_ref, drift_ref, even_ref, odd_ref, sems,
):
    fetches = []
    for ref, first, place in ((row_ref, 4, RAW), (row_ref, 18, RAW), (mid_ref, 5, STEPPED), (mid_ref, 17, STEPPED)):
        fetches.append(
            pltpu.make_async_copy(
                kept_in.at[place + first : place + first + 2], ref.at[first : first + 2], sems.at[len(fetches)]
            )
        )
        fetches[-1].start()
    odd = place_ref[3] == 1
    unpack_state(lambda source: jnp.where(odd, near_ref[source], far_ref[source]), row_ref, 0)
    unpack_state(lambda source: jnp.where(odd, far_ref[source], near_ref[source]), row_ref, 5)
    for copy in fetches:
        copy.wait()
    expand(row_ref, 1, 6, drift_ref)
    expand(row_ref, 18, 23, drift_ref)
    copies = []

    def keep(ref, first, last, place):
        copy = pltpu.make_async_copy(
            ref.at[first:last], kept_out.at[place + first : place + last], sems.at[4 + len(copies)]
        )
        copy.start()
        copies.append(copy)

    keep(drift_ref, 3, 4, DRIFT)
    keep(drift_ref, 20, 21, DRIFT)
    moved_rows(row_ref, drift_ref, even_ref, odd_ref, 1, 5, 0)
    moved_rows(row_ref, drift_ref, even_ref, odd_ref, 19, 23, 4)
    filtered(even_ref, odd_ref, basis_ref, resp_ref, [(1, 5), (19, 23)], mid_ref)
    moved_rows(mid_ref, drift_ref, even_ref, odd_ref, 2, 6, 0)
    moved_rows(mid_ref, drift_ref, even_ref, odd_ref, 18, 22, 4)
    filtered(even_ref, odd_ref, basis_ref, resp_ref, [(2, 6), (18, 22)], state_ref)
    keep(state_ref, 2, 6, STATE)
    keep(state_ref, 18, 22, STATE)
    for copy in copies:
        copy.wait()


def adjoint(place_ref, recv_ref, kept_in, traj_in, resp_ref, basis_ref, send_ref, held_ref, row_ref, field_ref, weight_ref, state_ref, drift_ref, even_ref, odd_ref, sems):
    held_copy = pltpu.make_async_copy(traj_in, held_ref, sems.at[2])
    state_copy = pltpu.make_async_copy(kept_in.at[0:BAND], state_ref, sems.at[0])
    state_copy.start()
    drift_copy = pltpu.make_async_copy(kept_in.at[BAND : 2 * BAND], drift_ref, sems.at[1])
    drift_copy.start()
    held_copy.start()
    for group in range(5):
        def load(source):
            return recv_ref[source, SENT * group : SENT * group + GROUP, :]

        def store(row, quarter, value):
            if group < 4:
                row_ref[4 * group + row + HALO, :, 128 * quarter : 128 * quarter + 128] = value
            else:
                at = 2 + row if row < 2 else 18 + row
                swapped = place_ref[1] if row < 2 else place_ref[2]
                lanes = pl.multiple_of(128 * ((quarter + 2 * swapped) & 3), 128)
                row_ref[at, :, pl.ds(lanes, 128)] = value

        unpack_rows(load, store)
    weight_ref[:, GROUP - 8 :, :] = jnp.zeros((BAND, 8, CYCLE), jnp.float32)
    for field in range(FIELDS):
        weight_ref[2:22, SHARE * field : SHARE * field + SHARE, :] = row_ref[2:22, PLANES : PLANES + SHARE, :]

    state_copy.wait()
    drift_copy.wait()

    def depart(index, carry):
        fold_store(even_ref, odd_ref, index - 2, weight_ref[index] * (state_ref[index] - row_ref[index]))
        return carry

    lax.fori_loop(2, 22, depart, 0, unroll=4)
    for step in range(2):
        first, last = 2 + step, BAND - 2 - step
        filtered(even_ref, odd_ref, basis_ref, resp_ref, [(first, last)], field_ref)

        def body(index, carry):
            here = field_ref[index]
            carried = drift_ref[index] * here
            spread = diffusion * here
            moved = here + diffusion * (field_ref[index - 1] + field_ref[index + 1] - 4.0 * here)
            moved = moved + pltpu.roll(spread + carried, 1, 1) + pltpu.roll(spread - carried, CYCLE - 1, 1)
            if step == 0:
                fold_store(even_ref, odd_ref, index - 3, moved)
            else:
                row_ref[index] = moved
            return carry

        lax.fori_loop(first + 1, last - 1, body, 0, unroll=4)
    block = lane_block()
    for group in range(4):
        for quarter in range(4):
            lanes = slice(128 * quarter, 128 * quarter + 128)
            pieces = [row_ref[HALO + 4 * group + row, :, lanes] for row in range(4)]
            for source in range(4):
                value = turn(pieces[0], -source)
                for row in range(1, 4):
                    value = jnp.where(block == row, turn(pieces[row], row - source), value)
                send_ref[4 * quarter + source, PLANES * group : PLANES * group + PLANES, :] = value[:PLANES]
    held_copy.wait()


def prolong(place_ref, back_ref, cost_ref, traj_ref, spread_ref, out_ref, wide_ref, slot_ref, sems):
    whole, rest = LEVELS // SHARE, LEVELS % SHARE

    upper = lax.broadcasted_iota(jnp.int32, (8, 128), 0) < 4

    def fill(owner, slot, levels):
        source = (owner + (WIDE // 2) * place_ref[0]) & (WIDE - 1)
        for group in range(4):
            change = (
                back_ref[source, SENT * group : SENT * group + PLANES, :]
                - cost_ref[source, PLANES * group : PLANES * group + PLANES, :]
            )
            high = change.astype(jnp.bfloat16)
            low = (change - high.astype(jnp.float32)).astype(jnp.bfloat16)
            spread = jnp.dot(
                jnp.concatenate([high, low], axis=1), spread_ref[...], preferred_element_type=jnp.float32
            )
            for part in range(4):
                wide_ref[4 * group + part, 0:PLANES, :] = spread[:, 128 * part : 128 * part + 128]
        for field in range(FIELDS):
            for level in range(levels):
                plane = field * SHARE + level
                rows = []
                for pair in range(8):
                    above = jnp.broadcast_to(wide_ref[2 * pair, plane : plane + 1, :], (8, 128))
                    below = jnp.broadcast_to(wide_ref[2 * pair + 1, plane : plane + 1, :], (8, 128))
                    rows.append(jnp.where(upper, above, below))
                fine = jnp.concatenate(rows, axis=0)
                first_guess = traj_ref[field, SHARE * owner + level].astype(jnp.float32)
                slot_ref[slot, field, level] = (first_guess + fine).astype(jnp.bfloat16)

    def copy(owner, slot, levels=SHARE):
        return pltpu.make_async_copy(
            slot_ref.at[slot, :, 0:levels], out_ref.at[:, pl.ds(SHARE * owner, levels)], sems.at[slot]
        )

    for owner in range(SLOTS):
        fill(owner, owner, SHARE)
        copy(owner, owner).start()

    def body(owner, carry):
        slot = owner & (SLOTS - 1)
        copy(owner - SLOTS, slot).wait()
        fill(owner, slot, SHARE)
        copy(owner, slot).start()
        return carry

    lax.fori_loop(SLOTS, whole, body, 0)
    slot = whole % SLOTS
    copy(whole - SLOTS, slot).wait()
    fill(whole, slot, rest)
    copy(whole, slot, rest).start()
    for owner in range(whole - SLOTS + 1, whole):
        copy(owner, owner % SLOTS).wait()
    copy(whole, slot, rest).wait()


def response_rows(narrow_index):
    row = narrow_index * ROWS - HALO + jnp.arange(BAND, dtype=jnp.int32)
    latitude = jnp.pi * ((row.astype(jnp.float32) + 0.5) / TOTAL_ROWS - 0.5)
    cutoff = 0.5 * CYCLE * jnp.cos(latitude)
    inside = (row >= 0) & (row < TOTAL_ROWS)
    cutoff = jnp.where(inside, cutoff, 1.0)
    scaled = jnp.asarray(WAVES, jnp.float32)[None, :] / cutoff[:, None]
    response = jnp.where(inside[:, None], 1.0 / (1.0 + scaled**4), 0.0)
    return response.reshape(BAND, 1, CYCLE)


def shards(trajectory, innovation, background, obs_weight):
    f32 = jnp.float32
    narrow_count = lax.axis_size("narrow")
    narrow_index = lax.axis_index("narrow")
    middle = narrow_count // 2
    near, far = [], []
    for row in range(narrow_count - 1):
        for lane in range(WIDE):
            other = (lane + WIDE // 2) % WIDE if row == middle - 1 else lane
            one, two = lane * narrow_count + row, other * narrow_count + row + 1
            swaps = near if row % 2 == 0 else far
            swaps += [(one, two), (two, one)]
    odd = narrow_index % 2 == 1
    place = jnp.stack([narrow_index >= middle, narrow_index == middle, narrow_index == middle - 1, odd]).astype(jnp.int32)
    innov = innovation.transpose(0, 2, 3, 1)
    back = background.transpose(0, 2, 3, 1)
    weight = obs_weight.transpose(1, 2, 0)
    basis = jnp.asarray(BASIS)
    response = response_rows(narrow_index)

    full = pl.BlockSpec(memory_space=pltpu.VMEM)
    away = pl.BlockSpec(memory_space=pltpu.HBM)
    small = pl.BlockSpec(memory_space=pltpu.SMEM)
    edge_shape = jax.ShapeDtypeStruct((FIELDS + 1, 2, COLS, LEVELS), f32)
    send_state, edge_near, edge_far = pl.pallas_call(
        pack_state,
        in_specs=[away] * 4,
        out_specs=[full, away, away],
        out_shape=[jax.ShapeDtypeStruct((WIDE * STATE_ROWS, 128), f32), edge_shape, edge_shape],
        scratch_shapes=[
            pltpu.VMEM((24, 80, 128), f32),
            pltpu.VMEM((LEVELS * PITCH, 128), f32),
            pltpu.VMEM((FIELDS, ROWS, COLS, LEVELS), f32),
            pltpu.VMEM((LEVELS, 64, 128), jnp.bfloat16),
            pltpu.VMEM((2, FIELDS + 1, 2, COLS, LEVELS), f32),
            pltpu.SemaphoreType.DMA((FIELDS + 7,)),
        ],
        compiler_params=params(60),
        cost_estimate=estimate(3),
    )(back, trajectory, innov, weight)
    edge_near = lax.ppermute(edge_near, ("wide", "narrow"), near)
    edge_far = lax.ppermute(edge_far, ("wide", "narrow"), far)
    send_state = send_state.reshape(WIDE, STATE_ROWS, 128)
    held_state = lax.all_to_all(send_state, "wide", split_axis=0, concat_axis=0, tiled=True)

    send_depart = pl.pallas_call(
        pack_departures,
        in_specs=[small] + [full] * 4,
        out_specs=full,
        out_shape=jax.ShapeDtypeStruct((WIDE * DEPART_ROWS, 128), f32),
        scratch_shapes=[pltpu.VMEM((30, 80, 128), f32)],
        compiler_params=params(16),
        cost_estimate=estimate(3),
    )(place, innov, weight, edge_near, edge_far)
    send_depart = send_depart.reshape(WIDE, DEPART_ROWS, 128)

    first, last = held_state[:, :GROUP], held_state[:, STATE_ROWS - GROUP :]
    rows_near = lax.ppermute(jnp.where(odd, first, last), ("wide", "narrow"), near)
    rows_far = lax.ppermute(jnp.where(odd, last, first), ("wide", "narrow"), far)
    held_depart = lax.all_to_all(send_depart, "wide", split_axis=0, concat_axis=0, tiled=True)

    rows_shape = (BAND, GROUP, CYCLE)
    folded = pltpu.VMEM(((BAND - 2) * GROUP, CYCLE), jnp.bfloat16)
    kept_shape = jax.ShapeDtypeStruct((KEPT, GROUP, CYCLE), f32)
    kept = pl.pallas_call(
        tangent,
        in_specs=[full] * 3,
        out_specs=away,
        out_shape=kept_shape,
        scratch_shapes=[pltpu.VMEM(rows_shape, f32)] * 4 + [folded, folded, pltpu.SemaphoreType.DMA((6,))],
        compiler_params=params(40),
        cost_estimate=estimate(5),
    )(held_state, response, basis)
    kept = pl.pallas_call(
        tangent_edges,
        in_specs=[small] + [full] * 4 + [away],
        out_specs=away,
        out_shape=kept_shape,
        input_output_aliases={5: 0},
        scratch_shapes=[pltpu.VMEM(rows_shape, f32)] * 4 + [folded, folded, pltpu.SemaphoreType.DMA((8,))],
        compiler_params=params(40),
        cost_estimate=estimate(3),
    )(place, rows_near, rows_far, response, basis, kept)
    send_cost, held = pl.pallas_call(
        adjoint,
        in_specs=[small, full, away, away, full, full],
        out_specs=[full, full],
        out_shape=[
            jax.ShapeDtypeStruct((WIDE, 4 * PLANES, 128), f32),
            jax.ShapeDtypeStruct(trajectory.shape, jnp.bfloat16),
        ],
        scratch_shapes=[pltpu.VMEM(rows_shape, f32)] * 5 + [folded, folded, pltpu.SemaphoreType.DMA((3,))],
        compiler_params=params(40),
        cost_estimate=estimate(5),
    )(place, held_depart, kept, trajectory, response, basis)
    costate = lax.all_to_all(send_cost, "wide", split_axis=0, concat_axis=0, tiled=True)

    return pl.pallas_call(
        prolong,
        in_specs=[small] + [full] * 4,
        out_specs=away,
        out_shape=jax.ShapeDtypeStruct(trajectory.shape, jnp.bfloat16),
        scratch_shapes=[
            pltpu.VMEM((16, GROUP, 128), f32),
            pltpu.VMEM((SLOTS, FIELDS, SHARE, 64, 128), jnp.bfloat16),
            pltpu.SemaphoreType.DMA((SLOTS,)),
        ],
        compiler_params=params(24),
        cost_estimate=estimate(5),
    )(place, send_state, costate, held, jnp.asarray(spreading()))


def solution(mesh):
    in_specs = (
        P(None, None, "narrow", "wide"),
        P(None, None, "narrow", "wide"),
        P(None, None, "narrow", "wide"),
        P(None, "narrow", "wide"),
    )
    out_specs = P(None, None, "narrow", "wide")
    return jax.shard_map(shards, mesh=mesh, in_specs=in_specs, out_specs=out_specs, check_vma=False)
```
